32 devices in a mesh: tile: 16 (over z, y, core), mem: 2 (over x).
Axes of the slice: x: 2, y: 2, z: 4, core: 2. Of those that a mesh axis runs over, the one named last changes fastest.
Arguments:
- control: bfloat16 [4, 16, 768, 1536], P('mem', None, 'tile'), may hold values from -6 to 6
- members: bfloat16 [4, 16, 768, 1536], P('mem', None, 'tile'), may hold values from -6 to 6
- gradient: bfloat16 [16, 768, 1536], P('tile'), may hold values from -6 to 6
- step_x: float32 [1536], replicated, may hold values from 0.1 to 0.4
- step_y: float32 [768], replicated, may hold values from 0.01 to 0.1
- step_z: float32 [16], replicated, may hold values from 0.1 to 1
Outputs:
- increment: bfloat16 [16, 768, 1536], P('tile')
- control_grad: bfloat16 [4, 16, 768, 1536], P('mem', None, 'tile')
The draws below stay inside these ranges and needn't reach their ends.
All inputs are finite; a program needn't handle non-finite values.
Results may differ from the reference program's by a relative error of at most 0.0085.
Values may be sent and summed in bfloat16 or wider, within the bound.
No kernel may reach another device: no remote copies, remote signals or barrier semaphores. Data moves between devices by JAX's collectives and lax.ppermute only.
A program may use at most 128 MiB of HBM per device.

```python
import math
import jax
import jax.numpy as jnp
from jax import lax

NX = 1536
NY = 768
NZ = 16
MEMBERS = 4
BAND = 8


def shard_levels(rng, dims, split, least, high):
    factor_of = 1.0
    for axis_at, shards_of in split:
        steps = jax.random.uniform(jax.random.fold_in(jax.random.fold_in(rng, 6), axis_at), (shards_of,), jnp.float32, least / len(split), high / len(split))
        factor_of = factor_of * jnp.repeat(jnp.exp(steps), dims[axis_at] // shards_of).reshape((-1,) + (1,) * (len(dims) - 1 - axis_at))
    return factor_of


def centred(rng, shape, width, bound, shards=(), kind=jnp.bfloat16):
    level = shard_levels(rng, shape, shards, -0.22, 0.18) if shards else 1.0
    array = jax.random.normal(rng, shape, jnp.float32) * width * level
    return jnp.minimum(jnp.maximum(array, -bound), bound).astype(kind)


def setup_inputs(seed: int = 0) -> dict:
    streams_of = jax.random.split(jax.random.key(seed), 7)
    return {
        "control": centred(streams_of[0], (MEMBERS, NZ, NY, NX), 1.0, 6.0, ((0, 2), (2, 16))),
        "members": centred(streams_of[1], (MEMBERS, NZ, NY, NX), 1.0, 6.0, ((0, 2), (2, 16))),
        "gradient": centred(streams_of[2], (NZ, NY, NX), 1.0, 6.0, ((0, 16),)),
        "step_x": jnp.clip(jnp.exp(jax.random.uniform(streams_of[3], (NX,), jnp.float32, math.log(0.1), math.log(0.4))), 0.1, 0.4),
        "step_y": jnp.clip(jnp.exp(jax.random.uniform(streams_of[4], (NY,), jnp.float32, math.log(0.01), math.log(0.1))), 0.01, 0.1),
        "step_z": jnp.clip(jnp.exp(jax.random.uniform(streams_of[5], (NZ,), jnp.float32, math.log(0.1), math.log(1.0))), 0.1, 1.0),
    }


along_gain = 0.35
horiz_gain = 0.15
vert_gain = 0.5


def kernel_matrix(steps, gain):
    coord = jnp.cumsum(steps.astype(jnp.float32))
    return gain * jnp.exp(-jnp.abs(coord[:, None] - coord[None, :]))


def build_filters(step_x, step_y, step_z):
    filter_x = kernel_matrix(step_x, along_gain).astype(jnp.bfloat16)
    filter_y = kernel_matrix(step_y, horiz_gain).astype(jnp.bfloat16)
    level_ids = jnp.arange(step_z.shape[0], dtype=jnp.int32)
    banded = jnp.abs(level_ids[:, None] - level_ids[None, :]) <= BAND
    filter_z = jnp.where(banded, kernel_matrix(step_z, vert_gain), jnp.float32(0.0)).astype(jnp.bfloat16)
    return filter_x, filter_y, filter_z


def along_y(filter_y, field):
    return lax.map(lambda level: jnp.dot(filter_y, level, preferred_element_type=jnp.float32).astype(jnp.bfloat16), field)


def reference(control, members, gradient, step_x, step_y, step_z):
    filter_x, filter_y, filter_z = build_filters(step_x, step_y, step_z)
    grad_wide = gradient.astype(jnp.float32)

    def one_member(carry, pair):
        ctrl, memb = pair
        vert = jnp.dot(filter_z, ctrl.reshape(NZ, NY * NX), preferred_element_type=jnp.float32).astype(jnp.bfloat16)
        along = jnp.dot(vert.reshape(NZ * NY, NX), filter_x, preferred_element_type=jnp.float32).astype(jnp.bfloat16)
        shaped = along_y(filter_y, along.reshape(NZ, NY, NX))
        carry = carry + memb.astype(jnp.float32) * shaped.astype(jnp.float32)
        weighted = (memb.astype(jnp.float32) * grad_wide).astype(jnp.bfloat16)
        adj_y = along_y(filter_y, weighted)
        adj_x = jnp.dot(adj_y.reshape(NZ * NY, NX), filter_x, preferred_element_type=jnp.float32).astype(jnp.bfloat16)
        result = jnp.dot(filter_z.T, adj_x.reshape(NZ, NY * NX), preferred_element_type=jnp.float32).astype(jnp.bfloat16)
        return carry, result.reshape(NZ, NY, NX)

    total, grads = lax.scan(one_member, jnp.zeros((NZ, NY, NX), jnp.float32), (control, members))
    return total.astype(jnp.bfloat16), grads
```

```python
import functools

import jax
import jax.numpy as jnp
from jax import lax
from jax.experimental import pallas as pl
from jax.experimental.pallas import tpu as pltpu
from jax.sharding import PartitionSpec as P

BAND = 8

along_gain = 0.35
horiz_gain = 0.15
vert_gain = 0.5

BF16 = jnp.bfloat16
F32 = jnp.float32
VMEM_LIMIT = 48 * 1024 * 1024


def column_block(columns):
    for block in (256, 128):
        if columns % block == 0:
            return block
    return columns


def vertical_kernel(side_ref, mix_ref, mix_halo_ref, field_ref, halo_ref, memb_ref, out_ref):
    total = None
    for m in range(field_ref.shape[0]):
        shaped = jnp.dot(mix_ref[...], field_ref[m], preferred_element_type=F32)
        shaped += jnp.dot(mix_halo_ref[...], halo_ref[m], preferred_element_type=F32)
        term = shaped * memb_ref[m].astype(F32)
        total = term if total is None else total + term
    out_ref[...] = total.astype(out_ref.dtype)


def partial_increment(side, mix, mix_halo, field, halo, memb, kind):
    members, rows, columns = field.shape
    half = columns // 2
    block = column_block(half)
    steps = half // block
    pick = lambda j, side_ref: (0, 0, side_ref[0] * steps + j)
    return pl.pallas_call(
        vertical_kernel,
        grid_spec=pltpu.PrefetchScalarGridSpec(
            num_scalar_prefetch=1,
            grid=(steps,),
            in_specs=[
                pl.BlockSpec(mix.shape, lambda j, side_ref: (0, 0)),
                pl.BlockSpec(mix_halo.shape, lambda j, side_ref: (0, 0)),
                pl.BlockSpec((members, rows, block), pick),
                pl.BlockSpec((members, halo.shape[1], block), pick),
                pl.BlockSpec((members, rows, block), pick),
            ],
            out_specs=pl.BlockSpec((rows, block), lambda j, side_ref: (0, j)),
        ),
        out_shape=jax.ShapeDtypeStruct((rows, half), kind),
        compiler_params=pltpu.CompilerParams(vmem_limit_bytes=VMEM_LIMIT),
        cost_estimate=pl.CostEstimate(
            flops=2 * members * rows * (rows + halo.shape[1]) * half,
            bytes_accessed=2 * (2 * members * rows * half + rows * rows + rows * half),
            transcendentals=0,
        ),
        name="partial_increment",
    )(side, mix, mix_halo, field, halo, memb)


def adjoint_kernel(mix_ref, mix_halo_ref, field_ref, halo_ref, out_ref):
    total = jnp.dot(mix_ref[...], field_ref[...], preferred_element_type=F32)
    total += jnp.dot(mix_halo_ref[...], halo_ref[...], preferred_element_type=F32)
    out_ref[...] = total.astype(out_ref.dtype)


def adjoint_mix(mix, mix_halo, field, halo):
    members, rows, columns = field.shape
    block = column_block(columns)
    pick = lambda m, j: (m, 0, j)
    return pl.pallas_call(
        adjoint_kernel,
        grid=(members, columns // block),
        in_specs=[
            pl.BlockSpec(mix.shape, lambda m, j: (0, 0)),
            pl.BlockSpec(mix_halo.shape, lambda m, j: (0, 0)),
            pl.BlockSpec((None, rows, block), pick),
            pl.BlockSpec((None, halo.shape[1], block), pick),
        ],
        out_specs=pl.BlockSpec((None, rows, block), pick),
        out_shape=jax.ShapeDtypeStruct((members, rows, columns), BF16),
        compiler_params=pltpu.CompilerParams(vmem_limit_bytes=VMEM_LIMIT),
        cost_estimate=pl.CostEstimate(
            flops=2 * members * rows * (rows + halo.shape[1]) * columns,
            bytes_accessed=2 * (2 * members * rows * columns + rows * rows),
            transcendentals=0,
        ),
        name="adjoint_mix",
    )(mix, mix_halo, field, halo)


def body(tiles, control, members, gradient, step_x, step_y, step_z):
    count, levels, rows, columns = control.shape
    tile = lax.axis_index("tile")
    side = lax.axis_index("mem")
    coord_x = jnp.cumsum(step_x)
    coord_y = jnp.cumsum(step_y)
    coord_z = jnp.cumsum(step_z)
    filter_x = lax.optimization_barrier(
        (along_gain * jnp.exp(-jnp.abs(coord_x[:, None] - coord_x[None, :]))).astype(BF16)
    )

    level_gradient = gradient.reshape(gradient.shape[0] * tiles, rows, columns)
    if gradient.shape[0] > 1:
        level_gradient = (
            gradient.reshape(gradient.shape[0], tiles, rows, columns).swapaxes(0, 1)
        ).reshape(level_gradient.shape)
    row_gradient = lax.all_to_all(level_gradient, "tile", 0, 0, tiled=True)

    own_y = lax.dynamic_slice_in_dim(coord_y, tile * rows, rows)
    ends = coord_y.reshape(tiles, rows)[:, -1]
    starts = coord_y.reshape(tiles, rows)[:, 0]
    below = ends[jnp.maximum(tile - 1, 0)]
    above = starts[jnp.minimum(tile + 1, tiles - 1)]
    to_end = jnp.exp(own_y - own_y[-1])
    to_start = jnp.exp(own_y[0] - own_y)

    level_ids = jnp.arange(levels, dtype=jnp.int32)
    out_y, out_z, out_id = (
        jnp.tile(own_y, levels),
        jnp.repeat(coord_z, rows),
        jnp.repeat(level_ids, rows),
    )

    def mixing(in_y, in_z, in_id):
        distance = jnp.abs(out_y[:, None] - in_y[None, :]) + jnp.abs(out_z[:, None] - in_z[None, :])
        value = (horiz_gain * vert_gain) * jnp.exp(-distance)
        return jnp.where(jnp.abs(out_id[:, None] - in_id[None, :]) <= BAND, value, 0.0).astype(BF16)

    mix = mixing(out_y, out_z, out_id)
    mix_halo = mixing(
        jnp.concatenate([jnp.full((levels,), below), jnp.full((levels,), above)]),
        jnp.tile(coord_z, 2),
        jnp.tile(level_ids, 2),
    )
    mix, mix_halo = lax.optimization_barrier((mix, mix_halo))

    index = jnp.arange(tiles)
    weight_below = jnp.where(
        index[None, :] < index[:, None],
        jnp.exp(jnp.minimum(ends[None, :] - jnp.roll(ends, 1)[:, None], 0.0)),
        0.0,
    )
    weight_above = jnp.where(
        index[None, :] > index[:, None],
        jnp.exp(jnp.minimum(jnp.roll(starts, -1)[:, None] - starts[None, :], 0.0)),
        0.0,
    )

    def outside(fields):
        wide = fields.astype(F32)
        ending = jnp.sum(wide * to_end[None, None, :, None], axis=2).astype(BF16)
        starting = jnp.sum(wide * to_start[None, None, :, None], axis=2).astype(BF16)
        sums = jnp.stack([ending, starting], axis=0)
        sums = sums.transpose(2, 0, 1, 3)
        sums = lax.all_to_all(sums, "tile", 0, 0, tiled=True)
        sums = sums.reshape(tiles, levels // tiles, 2, count, columns).astype(F32)
        beyond = jnp.stack(
            [
                jnp.einsum("ts,slmx->tlmx", weight_below, sums[:, :, 0], precision="highest"),
                jnp.einsum("ts,slmx->tlmx", weight_above, sums[:, :, 1], precision="highest"),
            ],
            axis=2,
        ).astype(BF16)
        beyond = lax.all_to_all(
            beyond.reshape(levels, 2, count, columns), "tile", 0, 0, tiled=True
        )
        return beyond.transpose(2, 1, 0, 3).reshape(count, 2 * levels, columns)

    def filter_along_x(fields):
        flat = fields.reshape(-1, columns)
        return (
            jnp.dot(flat, filter_x, preferred_element_type=F32).astype(BF16).reshape(fields.shape)
        )

    flat = (count, levels * rows, columns)
    control_halo = filter_along_x(outside(control))
    along = filter_along_x(control.reshape(flat))
    memb = members.reshape(flat)
    sent = partial_increment((1 - side)[None], mix, mix_halo, along, control_halo, memb, BF16)
    kept = partial_increment(side[None], mix, mix_halo, along, control_halo, memb, F32)
    swap = [(0, 1), (1, 0)]
    other = lax.ppermute(sent, "mem", swap)
    half = (kept + other.astype(F32)).astype(BF16)
    half = lax.all_to_all(half.reshape(levels, rows, -1), "tile", 0, 0, tiled=True)
    half = half.reshape(tiles, levels // tiles, rows, -1).swapaxes(0, 1)
    half = half.reshape(levels // tiles, tiles * rows, -1)
    rest = lax.ppermute(half, "mem", swap)
    increment = jnp.where(
        side == 0,
        jnp.concatenate([half, rest], axis=2),
        jnp.concatenate([rest, half], axis=2),
    )

    weighted = (members.astype(F32) * row_gradient.astype(F32)[None]).astype(BF16)
    weighted_halo = filter_along_x(outside(weighted))
    adj_x = filter_along_x(weighted.reshape(flat))
    control_grad = adjoint_mix(mix, mix_halo, adj_x, weighted_halo).reshape(control.shape)
    return increment, control_grad


def solution(mesh):
    placed = (
        P("mem", None, "tile", None),
        P("mem", None, "tile", None),
        P("tile", None, None),
        P(),
        P(),
        P(),
    )
    return jax.shard_map(
        functools.partial(body, mesh.shape["tile"]),
        mesh=mesh,
        in_specs=placed,
        out_specs=(P("tile", None, None), P("mem", None, "tile", None)),
        check_vma=False,
    )
```

```python
import functools

import jax
import jax.numpy as jnp
from jax import lax
from jax.experimental import pallas as pl
from jax.experimental.pallas import tpu as pltpu
from jax.sharding import PartitionSpec as P

BAND = 8

along_gain = 0.35
horiz_gain = 0.15
vert_gain = 0.5

BF16 = jnp.bfloat16
F32 = jnp.float32
VMEM_LIMIT = 60 * 1024 * 1024
LANES = 128
SWAP = [(0, 1), (1, 0)]
CHUNKS = [3]


def params():
    return pltpu.CompilerParams(vmem_limit_bytes=VMEM_LIMIT)


def cost(flops, values):
    return pl.CostEstimate(flops=flops, bytes_accessed=2 * values, transcendentals=0)


def pick_block(size, *wanted):
    for block in wanted:
        if size % block == 0:
            return block
    return size


def dot(a, b):
    return jnp.dot(a, b, preferred_element_type=F32)


def prepare_x_kernel(block, step_ref, spread_ref, block_ref):
    columns = step_ref.shape[1]
    blocks = columns // block
    step = jnp.broadcast_to(step_ref[...], (block, columns))
    lane = lax.broadcasted_iota(jnp.int32, (block, columns), 1)
    row = lax.broadcasted_iota(jnp.int32, (block, columns), 0)
    edge = lax.broadcasted_iota(jnp.int32, (1, LANES), 1)
    firsts = jnp.where(edge < blocks, edge, edge - blocks) * block

    def to_row(col, first):
        eye = lax.broadcasted_iota(jnp.int32, (block, block), 0) == lax.broadcasted_iota(
            jnp.int32, (block, block), 1
        )
        return jnp.sum(jnp.where(eye, jnp.broadcast_to(col, (block, block)), 0.0), axis=0)[None]

    cols = []
    for b in range(blocks):
        cols.append(jnp.sum(jnp.where(lane <= row + b * block, step, 0.0), axis=1, keepdims=True))
    rows = [to_row(col, b * block) for b, col in enumerate(cols)]
    first = jnp.zeros((1, LANES), F32)
    last = jnp.zeros((1, LANES), F32)
    for b in range(blocks):
        first = jnp.where(edge == blocks + b, rows[b][:, :1], first)
        last = jnp.where(edge == b, rows[b][:, -1:], last)
    for b in range(blocks):
        near = dot_free_spread(cols[b], edge, blocks, b, first, last)
        spread_ref[b * block : (b + 1) * block, :] = near.astype(BF16)
        inside = along_gain * jnp.exp(-jnp.abs(cols[b] - rows[b]))
        block_ref[:block, b * block : (b + 1) * block] = inside.astype(BF16)
        which = lax.broadcasted_iota(jnp.int32, (LANES, block), 0)
        enter = jnp.zeros((LANES, block), F32)
        for a in range(blocks):
            if a < b:
                reach = rows[b] - rows[a][:, -1:]
                enter = jnp.where(which == a, jnp.exp(-reach), enter)
            if a > b:
                reach = rows[a][:, :1] - rows[b]
                enter = jnp.where(which == blocks + a, jnp.exp(-reach), enter)
        block_ref[block:, b * block : (b + 1) * block] = (along_gain * enter).astype(BF16)


def dot_free_spread(col, edge, blocks, b, first, last):
    to_last = jnp.exp(jnp.minimum(col - last, 0.0))
    to_first = jnp.exp(jnp.minimum(first - col, 0.0))
    return jnp.where(edge == b, to_last, 0.0) + jnp.where(edge == blocks + b, to_first, 0.0)


def prepare_x(step_x, block):
    columns = step_x.shape[0]
    return pl.pallas_call(
        functools.partial(prepare_x_kernel, block),
        out_shape=(
            jax.ShapeDtypeStruct((columns, LANES), BF16),
            jax.ShapeDtypeStruct((block + LANES, columns), BF16),
        ),
        compiler_params=params(),
        cost_estimate=cost(20 * columns * columns, 2 * columns * block),
        name="prepare_x",
    )(step_x[None])


def prepare_y_kernel(levels, tile_ref, step_y_ref, step_z_ref, mix_ref, halo_ref):
    size = mix_ref.shape[0]
    rows = size // levels
    base = tile_ref[0] * rows

    def split(shape, axis):
        index = lax.broadcasted_iota(jnp.int32, shape, axis)
        level = ((index.astype(F32) + 0.5) * (1.0 / rows)).astype(jnp.int32)
        return index, level, index - level * rows

    def coordinate(step_ref, upto):
        step = step_ref[...]
        shape = (upto.shape[0], step.shape[1])
        lane = lax.broadcasted_iota(jnp.int32, shape, 1)
        return jnp.sum(jnp.where(lane <= upto, jnp.broadcast_to(step, shape), 0.0), axis=1, keepdims=True)

    _, out_level, out_row = split((size, 1), 0)
    out_y = coordinate(step_y_ref, out_row + base)
    out_z = coordinate(step_z_ref, out_level)
    eye = lax.broadcasted_iota(jnp.int32, (size, size), 0) == lax.broadcasted_iota(
        jnp.int32, (size, size), 1
    )

    def to_row(col):
        return jnp.sum(jnp.where(eye, jnp.broadcast_to(col, (size, size)), 0.0), axis=0, keepdims=True)

    in_y = to_row(out_y)
    in_z = to_row(out_z)
    _, in_level, _ = split((1, size), 1)
    distance = jnp.abs(out_y - in_y) + jnp.abs(out_z - in_z)
    value = (horiz_gain * vert_gain) * jnp.exp(-distance)
    mix_ref[...] = jnp.where(jnp.abs(out_level - in_level) <= BAND, value, 0.0).astype(BF16)

    wide = 2 * levels
    column = lax.broadcasted_iota(jnp.int32, (1, wide), 1)
    halo_level = jnp.where(column < levels, column, column - levels)
    step_y = step_y_ref[...]
    lane = lax.broadcasted_iota(jnp.int32, step_y.shape, 1)
    below = jnp.sum(jnp.where(lane <= base - 1, step_y, 0.0), axis=1, keepdims=True)
    above = jnp.sum(jnp.where(lane <= base + rows, step_y, 0.0), axis=1, keepdims=True)
    step_z = step_z_ref[...]
    order = lax.broadcasted_iota(jnp.int32, (step_z.shape[1], wide), 0)
    turned = lax.broadcasted_iota(jnp.int32, (step_z.shape[1], step_z.shape[1]), 0)
    turned = turned == lax.broadcasted_iota(jnp.int32, turned.shape, 1)
    step_col = jnp.sum(jnp.where(turned, jnp.broadcast_to(step_z, turned.shape), 0.0), axis=1, keepdims=True)
    halo_z = jnp.sum(jnp.where(order <= halo_level, jnp.broadcast_to(step_col, order.shape), 0.0), axis=0, keepdims=True)
    reach = jnp.where(column < levels, out_y - below, above - out_y)
    value = (horiz_gain * vert_gain) * jnp.exp(-(jnp.abs(reach) + jnp.abs(out_z - halo_z)))
    halo_ref[...] = jnp.where(jnp.abs(out_level - halo_level) <= BAND, value, 0.0).astype(BF16)


def prepare_y(tile, step_y, step_z, levels, size):
    return pl.pallas_call(
        functools.partial(prepare_y_kernel, levels),
        grid_spec=pltpu.PrefetchScalarGridSpec(
            num_scalar_prefetch=1,
            grid=(1,),
            in_specs=[
                pl.BlockSpec((1, step_y.shape[0]), lambda i, t: (0, 0)),
                pl.BlockSpec((1, step_z.shape[0]), lambda i, t: (0, 0)),
            ],
            out_specs=[
                pl.BlockSpec((size, size), lambda i, t: (0, 0)),
                pl.BlockSpec((size, 2 * levels), lambda i, t: (0, 0)),
            ],
        ),
        out_shape=[
            jax.ShapeDtypeStruct((size, size), BF16),
            jax.ShapeDtypeStruct((size, 2 * levels), BF16),
        ],
        compiler_params=params(),
        cost_estimate=cost(20 * size * size, size * size),
        name="prepare_y",
    )(tile[None], step_y[None], step_z[None])


def edge_kernel(levels, rows, tile_ref, step_ref, field_ref, edge_ref, out_ref):
    @pl.when(jnp.logical_and(pl.program_id(0) == 0, pl.program_id(1) == 0))
    def _():
        base = tile_ref[0] * rows
        steps = step_ref.shape[1]
        size = edge_ref.shape[1]
        at = lax.broadcasted_iota(jnp.int32, (rows, steps), 1) - base
        row = lax.broadcasted_iota(jnp.int32, (rows, steps), 0)
        step = jnp.broadcast_to(step_ref[...], (rows, steps))
        own = jnp.sum(jnp.where(jnp.logical_and(at == row, row > 0), step, 0.0), axis=1, keepdims=True)
        column = lax.broadcasted_iota(jnp.int32, (1, size), 1)
        level = ((column.astype(F32) + 0.5) * (1.0 / rows)).astype(jnp.int32)
        row = lax.broadcasted_iota(jnp.int32, (rows, size), 0)
        reached = jnp.where(row <= column - level * rows, jnp.broadcast_to(own, (rows, size)), 0.0)
        from_first = jnp.sum(reached, axis=0, keepdims=True)
        to_last = jnp.sum(own, axis=0, keepdims=True) - from_first
        which = lax.broadcasted_iota(jnp.int32, (2 * levels, 1), 0)
        ending = which < levels
        reach = jnp.where(ending, to_last, from_first)
        own_level = jnp.where(ending, which, which - levels) == level
        edge_ref[...] = jnp.where(own_level, jnp.exp(-jnp.abs(reach)), 0.0).astype(BF16)

    out_ref[...] = dot(edge_ref[...], field_ref[...]).astype(BF16)


def edge_sums(tile, step_y, levels, field):
    count, size, columns = field.shape
    block = pick_block(columns, 768, 256, 128)
    return pl.pallas_call(
        functools.partial(edge_kernel, levels, size // levels),
        grid_spec=pltpu.PrefetchScalarGridSpec(
            num_scalar_prefetch=1,
            grid=(count, columns // block),
            in_specs=[
                pl.BlockSpec((1, step_y.shape[0]), lambda m, j, t: (0, 0)),
                pl.BlockSpec((None, size, block), lambda m, j, t: (m, 0, j)),
            ],
            out_specs=[
                pl.BlockSpec((2 * levels, size), lambda m, j, t: (0, 0)),
                pl.BlockSpec((None, 2 * levels, block), lambda m, j, t: (m, 0, j)),
            ],
        ),
        out_shape=[
            jax.ShapeDtypeStruct((2 * levels, size), BF16),
            jax.ShapeDtypeStruct((count, 2 * levels, columns), BF16),
        ],
        compiler_params=params(),
        cost_estimate=cost(4 * levels * field.size, field.size),
        name="edge_sums",
    )(tile[None], step_y[None], field)


def weigh_kernel(edge_ref, memb_ref, grad_ref, after_ref, out_ref):
    out_ref[...] = dot(edge_ref[...], memb_ref[...] * grad_ref[...]).astype(BF16)


def weighted_edge_sums(edge, memb, grad, after):
    count, rows, columns = memb.shape
    block = pick_block(columns, 768, 256, 128)
    pick = lambda j, m: (m, 0, j)
    return pl.pallas_call(
        weigh_kernel,
        grid=(columns // block, count),
        in_specs=[
            pl.BlockSpec(edge.shape, lambda j, m: (0, 0)),
            pl.BlockSpec((None, rows, block), pick),
            pl.BlockSpec((rows, block), lambda j, m: (0, j)),
            pl.BlockSpec(memory_space=pl.ANY),
        ],
        out_specs=pl.BlockSpec((None, edge.shape[0], block), pick),
        out_shape=jax.ShapeDtypeStruct((count, edge.shape[0], columns), BF16),
        compiler_params=params(),
        cost_estimate=cost(2 * edge.shape[0] * memb.size, 2 * memb.size),
        name="weighted_edge_sums",
    )(edge, memb, grad, after)


def filter_x_kernel(block, field_ref, *refs):
    *weight, spread_ref, block_ref, after_ref, out_ref = refs
    field = field_ref[...]
    if weight:
        field = field * weight[0][...]
    edges = dot(field, spread_ref[...]).astype(BF16)
    for start in range(0, field.shape[1], block):
        part = slice(start, start + block)
        both = jnp.concatenate([field[:, part], edges], axis=1)
        out_ref[:, part] = dot(both, block_ref[:, part]).astype(BF16)


def filter_x(field, weight, spread_x, block_x, after):
    count, rows, columns = field.shape
    height = pick_block(rows, 384, 256, 128)
    block = block_x.shape[0] - LANES
    pick = lambda i, m: (m, i, 0)
    weights = () if weight is None else (weight,)
    return pl.pallas_call(
        functools.partial(filter_x_kernel, block),
        grid=(rows // height, count),
        in_specs=[
            pl.BlockSpec((None, height, columns), pick),
            *[pl.BlockSpec((height, columns), lambda i, m: (i, 0)) for _ in weights],
            pl.BlockSpec(spread_x.shape, lambda i, m: (0, 0)),
            pl.BlockSpec(block_x.shape, lambda i, m: (0, 0)),
            pl.BlockSpec(memory_space=pl.ANY),
        ],
        out_specs=pl.BlockSpec((None, height, columns), pick),
        out_shape=jax.ShapeDtypeStruct(field.shape, BF16),
        compiler_params=params(),
        cost_estimate=cost(2 * field.size * (block + 2 * LANES), 2 * field.size),
        name="filter_x",
    )(field, *weights, spread_x, block_x, after)


def halo_along_x(at, halo, sums, block_ref, block):
    part = halo[:, pl.ds(pl.multiple_of(at * block, block), block)]
    return dot(jnp.concatenate([part, sums], axis=1), block_ref[...]).astype(BF16)


def increment_kernel(
    block, side_ref, mix_ref, mix_halo_ref, field_ref, memb_ref, halo_ref, spread_ref, block_ref,
    out_ref, sums_ref,
):
    count = field_ref.shape[0]
    step = pl.program_id(0)

    @pl.when(step == 0)
    def _():
        for m in range(count):
            sums_ref[m] = dot(halo_ref[m], spread_ref[...]).astype(BF16)

    at = side_ref[0] + step
    total = None
    for m in range(count):
        halo = halo_along_x(at, halo_ref.at[m], sums_ref[m], block_ref, block)
        shaped = dot(mix_ref[...], field_ref[m]) + dot(mix_halo_ref[...], halo)
        term = shaped * memb_ref[m].astype(F32)
        total = term if total is None else total + term
    out_ref[...] = total.astype(out_ref.dtype)


def partial_increment(first, blocks, kind, mix, mix_halo, field, memb, halo, spread_x, block_x):
    count, rows, columns = field.shape
    block = block_x.shape[0] - LANES
    pick = lambda j, side: (0, 0, side[0] + j)
    whole2 = lambda j, side: (0, 0)
    return pl.pallas_call(
        functools.partial(increment_kernel, block),
        grid_spec=pltpu.PrefetchScalarGridSpec(
            num_scalar_prefetch=1,
            grid=(blocks,),
            in_specs=[
                pl.BlockSpec(mix.shape, whole2),
                pl.BlockSpec(mix_halo.shape, whole2),
                pl.BlockSpec((count, rows, block), pick),
                pl.BlockSpec((count, rows, block), pick),
                pl.BlockSpec(halo.shape, lambda j, side: (0, 0, 0)),
                pl.BlockSpec(spread_x.shape, whole2),
                pl.BlockSpec((block_x.shape[0], block), lambda j, side: (0, side[0] + j)),
            ],
            out_specs=pl.BlockSpec((rows, block), lambda j, side: (0, j)),
            scratch_shapes=[pltpu.VMEM((count, halo.shape[1], LANES), BF16)],
        ),
        out_shape=jax.ShapeDtypeStruct((rows, blocks * block), kind),
        compiler_params=params(),
        cost_estimate=cost(
            2 * count * rows * (rows + halo.shape[1]) * blocks * block,
            2 * count * rows * blocks * block + rows * rows,
        ),
        name="partial_increment",
    )(first[None], mix, mix_halo, field, memb, halo, spread_x, block_x)


def adjoint_kernel(
    block, mix_ref, mix_halo_ref, field_ref, halo_ref, spread_ref, block_ref, out_ref, sums_ref
):
    step = pl.program_id(1)
    wide = field_ref.shape[1] // block

    @pl.when(step == 0)
    def _():
        sums_ref[...] = dot(halo_ref[...], spread_ref[...]).astype(BF16)

    for k in range(wide):
        part = slice(k * block, (k + 1) * block)
        halo = halo_along_x(
            step * wide + k, halo_ref, sums_ref[...], block_ref.at[:, part], block
        )
        total = dot(mix_ref[...], field_ref[:, part]) + dot(mix_halo_ref[...], halo)
        out_ref[:, part] = total.astype(BF16)


def adjoint_mix(mix, mix_halo, field, halo, spread_x, block_x):
    count, rows, columns = field.shape
    block = block_x.shape[0] - LANES
    wide = pick_block(columns, 3 * block, 2 * block, block)
    pick = lambda m, j: (m, 0, j)
    whole2 = lambda m, j: (0, 0)
    return pl.pallas_call(
        functools.partial(adjoint_kernel, block),
        grid=(count, columns // wide),
        in_specs=[
            pl.BlockSpec(mix.shape, whole2),
            pl.BlockSpec(mix_halo.shape, whole2),
            pl.BlockSpec((None, rows, wide), pick),
            pl.BlockSpec((None,) + halo.shape[1:], lambda m, j: (m, 0, 0)),
            pl.BlockSpec(spread_x.shape, whole2),
            pl.BlockSpec((block_x.shape[0], wide), lambda m, j: (0, j)),
        ],
        out_specs=pl.BlockSpec((None, rows, wide), pick),
        out_shape=jax.ShapeDtypeStruct(field.shape, BF16),
        scratch_shapes=[pltpu.VMEM(halo.shape[1:2] + (LANES,), BF16)],
        compiler_params=params(),
        cost_estimate=cost(
            2 * rows * (rows + halo.shape[1]) * count * columns, 2 * field.size + rows * rows
        ),
        name="adjoint_mix",
    )(mix, mix_halo, field, halo, spread_x, block_x)


def exchange_factors(tile, tiles, rows, step_y):
    pairs = tiles // 2
    mine = tile - lax.rem(tile, 2)
    lasts = jnp.arange(1, pairs + 1, dtype=jnp.int32) * (2 * rows) - 1
    firsts = jnp.arange(pairs, dtype=jnp.int32) * (2 * rows)
    middle = (mine + 1) * rows
    start = mine * rows
    end = (mine + 2) * rows
    frm = jnp.concatenate(
        [jnp.stack([middle - 1, start, start - 1, (tile + 1) * rows]), lasts, jnp.full((pairs,), end)]
    )
    to = jnp.concatenate(
        [jnp.stack([end - 1, middle, tile * rows - 1, end]), jnp.full((pairs,), start - 1), firsts]
    )
    index = jnp.arange(step_y.shape[0], dtype=jnp.int32)[None]
    between = jnp.logical_and(index > frm[:, None], index <= to[:, None])
    return jnp.exp(-jnp.sum(jnp.where(between, step_y[None], 0.0), axis=1))


def outside(sums, tile, tiles, levels, factor, meanwhile):
    count, _, columns = sums.shape
    sums = sums.reshape(count, 2, levels, columns)
    part = count // 2
    pairs = tiles // 2
    odd = lax.rem(tile, 2)
    pair = lax.div(tile, 2)

    def swap(x):
        return lax.ppermute(x, "tile", [(s, s ^ 1) for s in range(tiles)])

    def by_way(up, down):
        return jnp.stack([up, down]).reshape(1, 2, 1, 1)

    other = swap(sums)
    one = jnp.float32(1.0)
    keep = by_way(jnp.where(odd == 1, one, factor[0]), jnp.where(odd == 1, factor[1], one))
    take = by_way(jnp.where(odd == 1, factor[0], one), jnp.where(odd == 1, one, factor[1]))
    mine = lax.dynamic_slice_in_dim(sums, odd * part, part, 0)
    theirs = lax.dynamic_slice_in_dim(other, odd * part, part, 0)
    group = (keep * mine.astype(F32) + take * theirs.astype(F32)).astype(BF16)
    index = jnp.arange(pairs, dtype=jnp.int32).reshape(pairs, 1, 1, 1)
    sent = jnp.where(index > pair, group[None, :, 0], group[None, :, 1])
    came = lax.all_to_all(
        sent, "tile", 0, 0, tiled=True,
        axis_index_groups=[list(range(c, tiles, 2)) for c in range(2)],
    )
    result = meanwhile(other)
    came, result = lax.optimization_barrier((came, result))
    came = came.astype(F32)
    weight = factor[4:].reshape(2, pairs, 1, 1, 1)
    below = jnp.sum(jnp.where(index < pair, weight[0] * came, 0.0), axis=0)
    above = jnp.sum(jnp.where(index > pair, weight[1] * came, 0.0), axis=0)
    far = jnp.stack([below, above], axis=1).astype(BF16)
    there = swap(far)
    far = jnp.where(
        odd == 0,
        jnp.concatenate([far, there], axis=0),
        jnp.concatenate([there, far], axis=0),
    )
    way = by_way(factor[2], factor[3])
    near = by_way(jnp.where(odd == 1, 1.0, 0.0), jnp.where(odd == 1, 0.0, 1.0))
    halo = (far.astype(F32) * way + other.astype(F32) * near).astype(BF16)
    return halo.reshape(count, 2 * levels, columns), result


def body(tiles, control, members, gradient, step_x, step_y, step_z):
    count, levels, rows, columns = control.shape
    flat = (count, levels * rows, columns)
    tile = lax.axis_index("tile")
    side = lax.axis_index("mem")
    half = columns // 2
    block = pick_block(half, 256, 128)
    owned = gradient.shape[0]

    mix, mix_halo = prepare_y(tile, step_y, step_z, levels, levels * rows)
    factor = exchange_factors(tile, tiles, rows, step_y)
    field = control.reshape(flat)
    memb = members.reshape(flat)
    edge, control_sums = edge_sums(tile, step_y, levels, field)

    level_gradient = gradient.reshape(owned, tiles, rows, columns).swapaxes(0, 1)
    row_gradient = lax.all_to_all(
        level_gradient.reshape(levels, rows, columns), "tile", 0, 0, tiled=True
    )

    spread_x, block_x = prepare_x(step_x, block)
    halo, along = outside(
        control_sums, tile, tiles, levels, factor,
        lambda after: filter_x(field, None, spread_x, block_x, after),
    )
    blocks = half // block
    share = functools.partial(
        partial_increment,
        mix=mix, mix_halo=mix_halo, field=along, memb=memb, halo=halo, spread_x=spread_x,
        block_x=block_x,
    )
    starts = [sum(CHUNKS[:k]) for k in range(len(CHUNKS))] if sum(CHUNKS) == blocks else [0]
    sizes = CHUNKS if sum(CHUNKS) == blocks else [blocks]
    sent = [share((1 - side) * blocks + at, size, BF16) for at, size in zip(starts, sizes)]
    others = [lax.ppermute(part, "mem", SWAP) for part in sent]
    kept = [share(side * blocks + at, size, F32) for at, size in zip(starts, sizes)]
    mine, rest = [], []
    for own, other in zip(kept, others):
        part = (own + other.astype(F32)).astype(BF16)
        part = lax.all_to_all(part.reshape(levels, rows, -1), "tile", 0, 0, tiled=True)
        part = part.reshape(tiles, owned, rows, -1).swapaxes(0, 1)
        mine.append(part.reshape(owned, tiles * rows, -1))
        rest.append(lax.ppermute(mine[-1], "mem", SWAP))
    increment = jnp.where(
        side == 0,
        jnp.concatenate(mine + rest, axis=2),
        jnp.concatenate(rest + mine, axis=2),
    )

    grad = row_gradient.reshape(flat[1:])
    weighted_sums = weighted_edge_sums(edge, memb, grad, sent[-1])
    weighted_halo, adj_x = outside(
        weighted_sums, tile, tiles, levels, factor,
        lambda after: filter_x(memb, grad, spread_x, block_x, after),
    )
    control_grad = adjoint_mix(mix, mix_halo, adj_x, weighted_halo, spread_x, block_x)
    return increment, control_grad.reshape(control.shape)


def solution(mesh):
    placed = (
        P("mem", None, "tile", None),
        P("mem", None, "tile", None),
        P("tile", None, None),
        P(),
        P(),
        P(),
    )
    return jax.shard_map(
        functools.partial(body, mesh.shape["tile"]),
        mesh=mesh,
        in_specs=placed,
        out_specs=(P("tile", None, None), P("mem", None, "tile", None)),
        check_vma=False,
    )
```

```python
import functools

import jax
import jax.numpy as jnp
import numpy as np
from jax import lax
from jax.experimental import pallas as pl
from jax.experimental.pallas import tpu as pltpu
from jax.sharding import PartitionSpec as P

BAND = 8

along_gain = 0.35
horiz_gain = 0.15
vert_gain = 0.5

BF16 = jnp.bfloat16
F32 = jnp.float32
VMEM_LIMIT = 60 * 1024 * 1024
LANES = 128
SWAP = [(0, 1), (1, 0)]
CHUNKS = [2, 1]


def params():
    return pltpu.CompilerParams(vmem_limit_bytes=VMEM_LIMIT)


def cost(flops, values):
    return pl.CostEstimate(flops=flops, bytes_accessed=2 * values, transcendentals=0)


def pick_block(size, *wanted):
    for block in wanted:
        if size % block == 0:
            return block
    return size


def dot(a, b):
    return jnp.dot(a, b, preferred_element_type=F32)


def prepare_x_kernel(block, step_ref, spread_ref, block_ref):
    columns = step_ref.shape[1]
    blocks = columns // block
    step = jnp.broadcast_to(step_ref[...], (block, columns))
    lane = lax.broadcasted_iota(jnp.int32, (block, columns), 1)
    row = lax.broadcasted_iota(jnp.int32, (block, columns), 0)
    edge = lax.broadcasted_iota(jnp.int32, (1, LANES), 1)
    firsts = jnp.where(edge < blocks, edge, edge - blocks) * block

    def to_row(col, first):
        eye = lax.broadcasted_iota(jnp.int32, (block, block), 0) == lax.broadcasted_iota(
            jnp.int32, (block, block), 1
        )
        return jnp.sum(jnp.where(eye, jnp.broadcast_to(col, (block, block)), 0.0), axis=0)[None]

    cols = []
    for b in range(blocks):
        cols.append(jnp.sum(jnp.where(lane <= row + b * block, step, 0.0), axis=1, keepdims=True))
    rows = [to_row(col, b * block) for b, col in enumerate(cols)]
    first = jnp.zeros((1, LANES), F32)
    last = jnp.zeros((1, LANES), F32)
    for b in range(blocks):
        first = jnp.where(edge == blocks + b, rows[b][:, :1], first)
        last = jnp.where(edge == b, rows[b][:, -1:], last)
    for b in range(blocks):
        near = dot_free_spread(cols[b], edge, blocks, b, first, last)
        spread_ref[b * block : (b + 1) * block, :] = near.astype(BF16)
        inside = along_gain * jnp.exp(-jnp.abs(cols[b] - rows[b]))
        block_ref[:block, b * block : (b + 1) * block] = inside.astype(BF16)
        which = lax.broadcasted_iota(jnp.int32, (LANES, block), 0)
        enter = jnp.zeros((LANES, block), F32)
        for a in range(blocks):
            if a < b:
                reach = rows[b] - rows[a][:, -1:]
                enter = jnp.where(which == a, jnp.exp(-reach), enter)
            if a > b:
                reach = rows[a][:, :1] - rows[b]
                enter = jnp.where(which == blocks + a, jnp.exp(-reach), enter)
        block_ref[block:, b * block : (b + 1) * block] = (along_gain * enter).astype(BF16)


def dot_free_spread(col, edge, blocks, b, first, last):
    to_last = jnp.exp(jnp.minimum(col - last, 0.0))
    to_first = jnp.exp(jnp.minimum(first - col, 0.0))
    return jnp.where(edge == b, to_last, 0.0) + jnp.where(edge == blocks + b, to_first, 0.0)


def prepare_x(step_x, block):
    columns = step_x.shape[0]
    return pl.pallas_call(
        functools.partial(prepare_x_kernel, block),
        out_shape=(
            jax.ShapeDtypeStruct((columns, LANES), BF16),
            jax.ShapeDtypeStruct((block + LANES, columns), BF16),
        ),
        compiler_params=params(),
        cost_estimate=cost(20 * columns * columns, 2 * columns * block),
        name="prepare_x",
    )(step_x[None])


def prepare_y_kernel(levels, tile_ref, step_y_ref, step_z_ref, after_ref, mix_ref, halo_ref, token_ref):
    size = mix_ref.shape[0]
    rows = size // levels
    base = tile_ref[0] * rows

    def split(shape, axis):
        index = lax.broadcasted_iota(jnp.int32, shape, axis)
        level = ((index.astype(F32) + 0.5) * (1.0 / rows)).astype(jnp.int32)
        return index, level, index - level * rows

    def coordinate(step_ref, upto):
        step = step_ref[...]
        shape = (upto.shape[0], step.shape[1])
        lane = lax.broadcasted_iota(jnp.int32, shape, 1)
        return jnp.sum(jnp.where(lane <= upto, jnp.broadcast_to(step, shape), 0.0), axis=1, keepdims=True)

    _, out_level, out_row = split((size, 1), 0)
    out_y = coordinate(step_y_ref, out_row + base)
    out_z = coordinate(step_z_ref, out_level)
    eye = lax.broadcasted_iota(jnp.int32, (size, size), 0) == lax.broadcasted_iota(
        jnp.int32, (size, size), 1
    )

    def to_row(col):
        return jnp.sum(jnp.where(eye, jnp.broadcast_to(col, (size, size)), 0.0), axis=0, keepdims=True)

    in_y = to_row(out_y)
    in_z = to_row(out_z)
    _, in_level, _ = split((1, size), 1)
    distance = jnp.abs(out_y - in_y) + jnp.abs(out_z - in_z)
    value = (horiz_gain * vert_gain) * jnp.exp(-distance)
    mix_ref[...] = jnp.where(jnp.abs(out_level - in_level) <= BAND, value, 0.0).astype(BF16)

    wide = 2 * levels
    column = lax.broadcasted_iota(jnp.int32, (1, wide), 1)
    halo_level = jnp.where(column < levels, column, column - levels)
    step_y = step_y_ref[...]
    lane = lax.broadcasted_iota(jnp.int32, step_y.shape, 1)
    below = jnp.sum(jnp.where(lane <= base - 1, step_y, 0.0), axis=1, keepdims=True)
    above = jnp.sum(jnp.where(lane <= base + rows, step_y, 0.0), axis=1, keepdims=True)
    step_z = step_z_ref[...]
    order = lax.broadcasted_iota(jnp.int32, (step_z.shape[1], wide), 0)
    turned = lax.broadcasted_iota(jnp.int32, (step_z.shape[1], step_z.shape[1]), 0)
    turned = turned == lax.broadcasted_iota(jnp.int32, turned.shape, 1)
    step_col = jnp.sum(jnp.where(turned, jnp.broadcast_to(step_z, turned.shape), 0.0), axis=1, keepdims=True)
    halo_z = jnp.sum(jnp.where(order <= halo_level, jnp.broadcast_to(step_col, order.shape), 0.0), axis=0, keepdims=True)
    reach = jnp.where(column < levels, out_y - below, above - out_y)
    value = (horiz_gain * vert_gain) * jnp.exp(-(jnp.abs(reach) + jnp.abs(out_z - halo_z)))
    halo_ref[...] = jnp.where(jnp.abs(out_level - halo_level) <= BAND, value, 0.0).astype(BF16)
    token_ref[...] = jnp.zeros_like(token_ref)


def prepare_y(tile, step_y, step_z, levels, size, after):
    return pl.pallas_call(
        functools.partial(prepare_y_kernel, levels),
        grid_spec=pltpu.PrefetchScalarGridSpec(
            num_scalar_prefetch=1,
            grid=(1,),
            in_specs=[
                pl.BlockSpec((1, step_y.shape[0]), lambda i, t: (0, 0)),
                pl.BlockSpec((1, step_z.shape[0]), lambda i, t: (0, 0)),
                pl.BlockSpec(memory_space=pl.ANY),
            ],
            out_specs=[
                pl.BlockSpec((size, size), lambda i, t: (0, 0)),
                pl.BlockSpec((size, 2 * levels), lambda i, t: (0, 0)),
                pl.BlockSpec((1, 2), lambda i, t: (0, 0)),
            ],
        ),
        out_shape=[
            jax.ShapeDtypeStruct((size, size), BF16),
            jax.ShapeDtypeStruct((size, 2 * levels), BF16),
            jax.ShapeDtypeStruct((1, 2), F32),
        ],
        compiler_params=params(),
        cost_estimate=cost(20 * size * size, size * size),
        name="prepare_y",
    )(tile[None], step_y[None], step_z[None], after)


def edge_kernel(levels, rows, tile_ref, step_ref, field_ref, edge_ref, out_ref):
    @pl.when(jnp.logical_and(pl.program_id(0) == 0, pl.program_id(1) == 0))
    def _():
        base = tile_ref[0] * rows
        steps = step_ref.shape[1]
        size = edge_ref.shape[1]
        at = lax.broadcasted_iota(jnp.int32, (rows, steps), 1) - base
        row = lax.broadcasted_iota(jnp.int32, (rows, steps), 0)
        step = jnp.broadcast_to(step_ref[...], (rows, steps))
        own = jnp.sum(jnp.where(jnp.logical_and(at == row, row > 0), step, 0.0), axis=1, keepdims=True)
        column = lax.broadcasted_iota(jnp.int32, (1, size), 1)
        level = ((column.astype(F32) + 0.5) * (1.0 / rows)).astype(jnp.int32)
        row = lax.broadcasted_iota(jnp.int32, (rows, size), 0)
        reached = jnp.where(row <= column - level * rows, jnp.broadcast_to(own, (rows, size)), 0.0)
        from_first = jnp.sum(reached, axis=0, keepdims=True)
        to_last = jnp.sum(own, axis=0, keepdims=True) - from_first
        which = lax.broadcasted_iota(jnp.int32, (2 * levels, 1), 0)
        ending = which < levels
        reach = jnp.where(ending, to_last, from_first)
        own_level = jnp.where(ending, which, which - levels) == level
        edge_ref[...] = jnp.where(own_level, jnp.exp(-jnp.abs(reach)), 0.0).astype(BF16)

    out_ref[...] = dot(edge_ref[...], field_ref[...]).astype(BF16)


def edge_sums(tile, step_y, levels, field):
    count, size, columns = field.shape
    block = pick_block(columns, 768, 256, 128)
    return pl.pallas_call(
        functools.partial(edge_kernel, levels, size // levels),
        grid_spec=pltpu.PrefetchScalarGridSpec(
            num_scalar_prefetch=1,
            grid=(count, columns // block),
            in_specs=[
                pl.BlockSpec((1, step_y.shape[0]), lambda m, j, t: (0, 0)),
                pl.BlockSpec((None, size, block), lambda m, j, t: (m, 0, j)),
            ],
            out_specs=[
                pl.BlockSpec((2 * levels, size), lambda m, j, t: (0, 0)),
                pl.BlockSpec((None, 2 * levels, block), lambda m, j, t: (m, 0, j)),
            ],
        ),
        out_shape=[
            jax.ShapeDtypeStruct((2 * levels, size), BF16),
            jax.ShapeDtypeStruct((count, 2 * levels, columns), BF16),
        ],
        compiler_params=params(),
        cost_estimate=cost(4 * levels * field.size, field.size),
        name="edge_sums",
    )(tile[None], step_y[None], field)


def weigh_kernel(edge_ref, memb_ref, grad_ref, after_ref, out_ref):
    out_ref[...] = dot(edge_ref[...], memb_ref[...] * grad_ref[...]).astype(BF16)


def weighted_edge_sums(which, edge, memb, grad, after):
    count, rows, columns = memb.shape
    half = columns // 2
    block = pick_block(half, 384, 256, 128)
    steps = half // block
    return pl.pallas_call(
        weigh_kernel,
        grid=(steps, count),
        in_specs=[
            pl.BlockSpec(edge.shape, lambda j, m: (0, 0)),
            pl.BlockSpec((None, rows, block), lambda j, m: (m, 0, which * steps + j)),
            pl.BlockSpec((rows, block), lambda j, m: (0, j)),
            pl.BlockSpec(memory_space=pl.ANY),
        ],
        out_specs=pl.BlockSpec((None, edge.shape[0], block), lambda j, m: (m, 0, j)),
        out_shape=jax.ShapeDtypeStruct((count, edge.shape[0], half), BF16),
        compiler_params=params(),
        cost_estimate=cost(edge.shape[0] * memb.size, memb.size),
        name="weighted_edge_sums",
    )(edge, memb, grad, after)


def filter_x_kernel(block, count, field_ref, *refs):
    weights, (spread_ref, block_ref), (out_ref, token_ref) = refs[:count], refs[count : count + 2], refs[-2:]
    field = field_ref[...]
    if weights:
        field = field * jnp.concatenate([ref[...] for ref in weights], axis=1)
    edges = dot(field, spread_ref[...]).astype(BF16)
    for start in range(0, field.shape[1], block):
        part = slice(start, start + block)
        both = jnp.concatenate([field[:, part], edges], axis=1)
        out_ref[:, part] = dot(both, block_ref[:, part]).astype(BF16)
    token_ref[...] = jnp.zeros_like(token_ref)


def filter_x(members, field, weights, spread_x, block_x, after):
    count, rows, columns = field.shape
    height = pick_block(rows, 384, 256, 128)
    block = block_x.shape[0] - LANES
    whole = lambda i, m: (0, 0)
    return pl.pallas_call(
        functools.partial(filter_x_kernel, block, len(weights)),
        grid=(rows // height, len(members)),
        in_specs=[
            pl.BlockSpec((None, height, columns), lambda i, m: (members[0] + m, i, 0)),
            *[pl.BlockSpec((height, columns // 2), lambda i, m: (i, 0)) for _ in weights],
            pl.BlockSpec(spread_x.shape, whole),
            pl.BlockSpec(block_x.shape, whole),
            *[pl.BlockSpec(memory_space=pl.ANY) for _ in after],
        ],
        out_specs=[
            pl.BlockSpec((None, height, columns), lambda i, m: (m, i, 0)),
            pl.BlockSpec((1, 2), whole),
        ],
        out_shape=[
            jax.ShapeDtypeStruct((len(members), rows, columns), BF16),
            jax.ShapeDtypeStruct((1, 2), F32),
        ],
        compiler_params=params(),
        cost_estimate=cost(
            2 * len(members) * rows * columns * (block + 2 * LANES), 2 * len(members) * rows * columns
        ),
        name="filter_x",
    )(field, *weights, spread_x, block_x, *after)


def halo_along_x(at, halo, sums, block_ref, block):
    part = halo[:, pl.ds(pl.multiple_of(at * block, block), block)]
    return dot(jnp.concatenate([part, sums], axis=1), block_ref[...]).astype(BF16)


def increment_kernel(
    block, slow, fast, where_ref, mix_ref, mix_halo_ref, memb_ref, halo_ref, spread_ref, block_ref,
    *refs
):
    count, size, _ = memb_ref.shape
    fields, outs, (sums_ref, mix_here, halo_here) = refs[:count], refs[-3 - fast : -3], refs[-3:]
    height = size // (slow * fast)
    step = pl.program_id(0)

    def owner(d, z):
        at = z * fast + lax.rem(where_ref[1] + d, fast)
        return pl.ds(pl.multiple_of(at * height, height), height)

    def place(d, z):
        return slice((d * slow + z) * height, (d * slow + z + 1) * height)

    @pl.when(step == 0)
    def _():
        for m in range(count):
            sums_ref[m] = dot(halo_ref[m], spread_ref[...]).astype(BF16)
        for d in range(fast):
            for z in range(slow):
                mix_here[place(d, z), :] = mix_ref[owner(d, z), :]
                halo_here[place(d, z), :] = mix_halo_ref[owner(d, z), :]

    at = where_ref[0] + step
    shaped = []
    for m in range(count):
        halo = halo_along_x(at, halo_ref.at[m], sums_ref[m], block_ref, block)
        shaped.append(dot(mix_here[...], fields[m][...]) + dot(halo_here[...], halo))
    for d in range(fast):
        for z in range(slow):
            total = None
            for m in range(count):
                term = shaped[m][place(d, z)] * memb_ref[m, owner(d, z), :].astype(F32)
                total = term if total is None else total + term
            outs[d][z * height : (z + 1) * height, :] = total.astype(BF16)


def partial_increment(
    first, after, blocks, place, slow, fast, mix, mix_halo, fields, memb, halo, spread_x, block_x
):
    count, rows, columns = memb.shape
    block = block_x.shape[0] - LANES
    pick = lambda j, w: (0, 0, w[0] + j)
    whole2 = lambda j, w: (0, 0)
    return pl.pallas_call(
        functools.partial(increment_kernel, block, slow, fast),
        grid_spec=pltpu.PrefetchScalarGridSpec(
            num_scalar_prefetch=1,
            grid=(blocks,),
            in_specs=[
                pl.BlockSpec(mix.shape, whole2),
                pl.BlockSpec(mix_halo.shape, whole2),
                pl.BlockSpec((count, rows, block), pick),
                pl.BlockSpec(halo.shape, lambda j, w: (0, 0, 0)),
                pl.BlockSpec(spread_x.shape, whole2),
                pl.BlockSpec((block_x.shape[0], block), lambda j, w: (0, w[0] + j)),
                *[pl.BlockSpec((None, rows, block), pick) for _ in fields],
                *[pl.BlockSpec(memory_space=pl.ANY) for _ in after],
            ],
            out_specs=[pl.BlockSpec((rows // fast, block), lambda j, w: (0, j))] * fast,
            scratch_shapes=[
                pltpu.VMEM((count, halo.shape[1], LANES), BF16),
                pltpu.VMEM(mix.shape, BF16),
                pltpu.VMEM(mix_halo.shape, BF16),
            ],
        ),
        out_shape=[jax.ShapeDtypeStruct((rows // fast, blocks * block), BF16)] * fast,
        compiler_params=params(),
        cost_estimate=cost(
            2 * count * rows * (rows + halo.shape[1]) * blocks * block,
            2 * count * rows * blocks * block + rows * rows,
        ),
        name="partial_increment",
    )(jnp.stack([first, place]), mix, mix_halo, memb, halo, spread_x, block_x, *fields, *after)


def join_kernel(slow, fast, layer_ref, *refs):
    own, other, outs = refs[:fast], refs[fast : 2 * fast], refs[-slow:]
    height = own[0].shape[0] // slow
    for d in range(slow):
        z = lax.rem(layer_ref[0] + d, slow)
        rows = pl.ds(pl.multiple_of(z * height, height), height)
        for k in range(fast):
            total = own[k][rows, :].astype(F32) + other[k][rows, :].astype(F32)
            outs[d][k * height : (k + 1) * height, :] = total.astype(BF16)


def join(layer, slow, fast, own, other, after):
    rows, columns = own[0].shape
    block = pick_block(columns, 384, 256, 128)
    pick = lambda j, layer: (0, j)
    height = rows // slow
    return pl.pallas_call(
        functools.partial(join_kernel, slow, fast),
        grid_spec=pltpu.PrefetchScalarGridSpec(
            num_scalar_prefetch=1,
            grid=(columns // block,),
            in_specs=[pl.BlockSpec((rows, block), pick)] * (2 * fast)
            + [pl.BlockSpec(memory_space=pl.ANY)],
            out_specs=[pl.BlockSpec((fast * height, block), pick)] * slow,
        ),
        out_shape=[jax.ShapeDtypeStruct((fast * height, columns), BF16)] * slow,
        compiler_params=params(),
        cost_estimate=cost(fast * rows * columns, 3 * fast * rows * columns),
        name="join",
    )(layer[None], *own, *other, after)


def hold_kernel(*refs):
    del refs


def hold(array, *after):
    return pl.pallas_call(
        hold_kernel,
        in_specs=[pl.BlockSpec(memory_space=pl.ANY)] * (1 + len(after)),
        out_specs=pl.BlockSpec(memory_space=pl.ANY),
        out_shape=jax.ShapeDtypeStruct(array.shape, array.dtype),
        input_output_aliases={0: 0},
        name="hold",
    )(array, *after)


def adjoint_inside_kernel(mix_ref, memb_ref, grad_ref, after_ref, out_ref, token_ref):
    token_ref[...] = jnp.zeros_like(token_ref)
    out_ref[...] = dot(mix_ref[...], memb_ref[...] * grad_ref[...]).astype(BF16)


def adjoint_inside(which, mix, memb, grad, after):
    count, rows, columns = memb.shape
    half = columns // 2
    block = pick_block(half, 384, 256, 128)
    steps = half // block
    return pl.pallas_call(
        adjoint_inside_kernel,
        grid=(steps, count),
        in_specs=[
            pl.BlockSpec(mix.shape, lambda j, m: (0, 0)),
            pl.BlockSpec((None, rows, block), lambda j, m: (m, 0, which * steps + j)),
            pl.BlockSpec((rows, block), lambda j, m: (0, j)),
            pl.BlockSpec(memory_space=pl.ANY),
        ],
        out_specs=[
            pl.BlockSpec((None, rows, block), lambda j, m: (m, 0, j)),
            pl.BlockSpec((1, 2), lambda j, m: (0, 0)),
        ],
        out_shape=[
            jax.ShapeDtypeStruct((count, rows, half), BF16),
            jax.ShapeDtypeStruct((1, 2), F32),
        ],
        compiler_params=params(),
        cost_estimate=cost(rows * memb.size, memb.size + rows * rows),
        name="adjoint_inside",
    )(mix, memb, grad, after)


def adjoint_kernel(
    block, left_ref, right_ref, mix_halo_ref, halo_ref, spread_ref, block_ref, out_ref
):
    inside = jnp.concatenate([left_ref[...], right_ref[...]], axis=1)
    field = (dot(mix_halo_ref[...], halo_ref[...]) + inside.astype(F32)).astype(BF16)
    edges = dot(field, spread_ref[...]).astype(BF16)
    for start in range(0, field.shape[1], block):
        part = slice(start, start + block)
        both = jnp.concatenate([field[:, part], edges], axis=1)
        out_ref[:, part] = dot(both, block_ref[:, part]).astype(BF16)


def adjoint_outside(left, right, mix_halo, halo, spread_x, block_x):
    count, rows, half = left.shape
    height = pick_block(rows, 384, 256, 128)
    block = block_x.shape[0] - LANES
    pick = lambda m, i: (m, i, 0)
    whole = lambda m, i: (0, 0)
    return pl.pallas_call(
        functools.partial(adjoint_kernel, block),
        grid=(count, rows // height),
        in_specs=[
            pl.BlockSpec((None, height, half), pick),
            pl.BlockSpec((None, height, half), pick),
            pl.BlockSpec((height, mix_halo.shape[1]), lambda m, i: (i, 0)),
            pl.BlockSpec((None,) + halo.shape[1:], lambda m, i: (m, 0, 0)),
            pl.BlockSpec(spread_x.shape, whole),
            pl.BlockSpec(block_x.shape, whole),
        ],
        out_specs=pl.BlockSpec((None, height, 2 * half), pick),
        out_shape=jax.ShapeDtypeStruct((count, rows, 2 * half), BF16),
        compiler_params=params(),
        cost_estimate=cost(4 * left.size * (block + 2 * LANES), 4 * left.size),
        name="adjoint_outside",
    )(left, right, mix_halo, halo, spread_x, block_x)


def hop_factors(tile, tiles, rows, step_y):
    hops = np.array([1 << k for k in range(tiles.bit_length() - 1)], np.int32)
    pair = tile - lax.rem(tile, 2)
    group = tile - lax.rem(jnp.broadcast_to(tile, hops.shape), hops)
    upper = lax.rem(lax.div(group, hops), np.int32(2)) == 1
    first = jnp.where(upper, group - hops, group)
    middle = first + hops
    base = jnp.where(hops == 1, tile, pair)
    after = jnp.where(hops == 1, tile + 1, pair + 2)
    frm = [middle * rows - 1, first * rows, middle * rows - 1, after * rows]
    to = [(middle + hops) * rows - 1, middle * rows, base * rows - 1, middle * rows]
    frm = jnp.concatenate(frm + [jnp.stack([pair * rows - 1, (tile + 1) * rows])])
    to = jnp.concatenate(to + [jnp.stack([tile * rows - 1, (pair + 2) * rows])])
    index = jnp.arange(step_y.shape[0], dtype=jnp.int32)[None]
    between = jnp.logical_and(index > frm[:, None], index <= to[:, None])
    factor = jnp.exp(-jnp.sum(jnp.where(between, step_y[None], 0.0), axis=1))
    end, start, below, above = [factor[k * len(hops) : (k + 1) * len(hops)] for k in range(4)]
    upper = upper.astype(F32)
    lower = 1.0 - upper
    ways = [
        upper + lower * end, upper * start + lower,
        upper * end + lower, upper + lower * start,
        upper * below, lower * above,
    ]
    return jnp.stack(ways, axis=1).reshape(len(hops), 3, 2), factor[4 * len(hops) :]


def outside(sums, tile, tiles, levels, factors, meanwhile):
    count, _, columns = sums.shape
    sums = sums.reshape(count, 2, levels, columns)
    part = count // 2
    odd = lax.rem(tile, 2)
    factor, way = factors

    def pair(x, hop):
        return lax.ppermute(x, "tile", [(s, s ^ hop) for s in range(tiles)])

    def by_way(pair_of):
        return pair_of.reshape(1, 2, 1, 1)

    other = pair(sums, 1)
    mine = lax.dynamic_slice_in_dim(sums, odd * part, part, 0).astype(F32)
    theirs = lax.dynamic_slice_in_dim(other, odd * part, part, 0).astype(F32)
    group = (by_way(factor[0, 0]) * mine + by_way(factor[0, 1]) * theirs).astype(BF16)
    token = meanwhile(0, other)
    far = jnp.zeros(group.shape, F32)
    hop, at = 2, 1
    while hop < tiles:
        enter = factor[at, 2]
        if 2 * hop < tiles:
            theirs = pair(group, hop)
            came = theirs
            keep = factor[at, 0]
            if token is not None:
                keep = keep + token[0]
            group = by_way(keep) * group.astype(F32) + by_way(factor[at, 1]) * theirs.astype(F32)
            group = group.astype(BF16)
        else:
            upper = lax.rem(lax.div(tile, hop), 2) == 1
            theirs = pair(jnp.where(upper, group[:, 1], group[:, 0]), hop)
            came = theirs[:, None]
            if token is not None:
                enter = enter + token[0]
        far += by_way(enter) * came.astype(F32)
        token = meanwhile(at, theirs)
        hop *= 2
        at += 1
    far = far.astype(BF16)
    there = pair(far, 1)
    far = jnp.where(
        odd == 0,
        jnp.concatenate([far, there], axis=0),
        jnp.concatenate([there, far], axis=0),
    )
    halo = far.astype(F32) * by_way(way) + other.astype(F32) * by_way(factor[0, 2])
    return halo.astype(BF16).reshape(count, 2 * levels, columns), theirs


def body(tiles, control, members, gradient, step_x, step_y, step_z):
    count, levels, rows, columns = control.shape
    flat = (count, levels * rows, columns)
    tile = lax.axis_index("tile")
    side = lax.axis_index("mem")
    half = columns // 2
    block = pick_block(half, 256, 128)
    owned = gradient.shape[0]
    def in_order(own, other, axis):
        return jnp.where(
            side == 0,
            jnp.concatenate([own, other], axis=axis),
            jnp.concatenate([other, own], axis=axis),
        )

    def to_rows(part):
        part = part.reshape(owned, tiles, rows, -1).swapaxes(0, 1).reshape(levels, rows, -1)
        return lax.all_to_all(part, "tile", 0, 0, tiled=True).reshape(levels * rows, -1)

    def to_levels(part):
        part = lax.all_to_all(part.reshape(levels, rows, -1), "tile", 0, 0, tiled=True)
        part = part.reshape(tiles, owned, rows, -1).swapaxes(0, 1)
        return part.reshape(owned, tiles * rows, -1)

    left = to_rows(gradient[:, :, :half])

    factors = hop_factors(tile, tiles, rows, step_y)
    field = control.reshape(flat)
    memb = members.reshape(flat)
    edge, control_sums = edge_sums(tile, step_y, levels, field)
    spread_x, block_x = prepare_x(step_x, block)
    along, mixes = [], []

    def prepare(k, came):
        if k < count:
            result, token = filter_x([k], field, (), spread_x, block_x, (came,))
            along.append(result)
            return token
        if k == count:
            *result, token = prepare_y(tile, step_y, step_z, levels, levels * rows, came)
            mixes.extend(result)
            return token
        return None

    halo, last = outside(control_sums, tile, tiles, levels, factors, prepare)
    for k in range(len(along) + len(mixes) // 2, count + 1):
        prepare(k, last)
    mix, mix_halo = mixes

    right = to_rows(hold(gradient[:, :, half:], last, mix))

    blocks = half // block
    sizes = CHUNKS if sum(CHUNKS) == blocks else [blocks]
    starts = [sum(sizes[:k]) for k in range(len(sizes))]
    share = functools.partial(
        partial_increment,
        place=jnp.int32(0), slow=1, fast=1, mix=mix, mix_halo=mix_halo, fields=along, memb=memb,
        halo=halo, spread_x=spread_x, block_x=block_x,
    )
    sent, kept = [], []
    for at, size in zip(starts, sizes):
        sent += share((1 - side) * blocks + at, sent[-1:], blocks=size)
    others = [lax.ppermute(x, "mem", SWAP) for x in sent]
    left_sums = weighted_edge_sums(0, edge, memb, left, sent[-1])
    now, mine, rest = left_sums, [], []
    for k, (at, size) in enumerate(zip(starts, sizes)):
        (own,) = share(side * blocks + at, [now], blocks=size)
        now = own
        if k == 0:
            now = right_sums = weighted_edge_sums(1, edge, memb, right, now)
        if k == len(sizes) - 1:
            left_inside, _ = adjoint_inside(0, mix, memb, left, now)
            now = left_inside
        (now,) = join(jnp.int32(0), 1, 1, [own], [others[k]], now)
        mine.append(to_levels(now))
        rest.append(lax.ppermute(mine[-1], "mem", SWAP))
    increment = in_order(jnp.concatenate(mine, axis=2), jnp.concatenate(rest, axis=2), 2)

    hops = tiles.bit_length() - 1
    right_inside = []

    def work(k, came):
        if k != hops - 2:
            return None
        result, token = adjoint_inside(1, mix, memb, right, now)
        right_inside.append(result)
        return token

    weighted_sums = jnp.concatenate([left_sums, right_sums], axis=2)
    weighted_halo, _ = outside(weighted_sums, tile, tiles, levels, factors, work)
    control_grad = adjoint_outside(
        left_inside, right_inside[0], mix_halo, weighted_halo, spread_x, block_x
    )
    return increment, control_grad.reshape(control.shape)


def solution(mesh):
    placed = (
        P("mem", None, "tile", None),
        P("mem", None, "tile", None),
        P("tile", None, None),
        P(),
        P(),
        P(),
    )
    return jax.shard_map(
        functools.partial(body, mesh.shape["tile"]),
        mesh=mesh,
        in_specs=placed,
        out_specs=(P("tile", None, None), P("mem", None, "tile", None)),
        check_vma=False,
    )
```

```python
import functools

import jax
import jax.numpy as jnp
import numpy as np
from jax import lax
from jax.experimental import pallas as pl
from jax.experimental.pallas import tpu as pltpu
from jax.sharding import PartitionSpec as P

BAND = 8

along_gain = 0.35
horiz_gain = 0.15
vert_gain = 0.5

BF16 = jnp.bfloat16
F32 = jnp.float32
VMEM_LIMIT = 60 * 1024 * 1024
LANES = 128
SWAP = [(0, 1), (1, 0)]
CHUNKS = [2, 1]


def params():
    return pltpu.CompilerParams(vmem_limit_bytes=VMEM_LIMIT)


def cost(flops, values):
    return pl.CostEstimate(flops=flops, bytes_accessed=2 * values, transcendentals=0)


def pick_block(size, *wanted):
    for block in wanted:
        if size % block == 0:
            return block
    return size


def dot(a, b):
    return jnp.dot(a, b, preferred_element_type=F32)


def prepare_x_kernel(block, step_ref, after_ref, spread_ref, block_ref):
    columns = step_ref.shape[1]
    blocks = columns // block
    step = jnp.broadcast_to(step_ref[...], (block, columns))
    lane = lax.broadcasted_iota(jnp.int32, (block, columns), 1)
    row = lax.broadcasted_iota(jnp.int32, (block, columns), 0)
    edge = lax.broadcasted_iota(jnp.int32, (1, LANES), 1)
    firsts = jnp.where(edge < blocks, edge, edge - blocks) * block

    def to_row(col, first):
        eye = lax.broadcasted_iota(jnp.int32, (block, block), 0) == lax.broadcasted_iota(
            jnp.int32, (block, block), 1
        )
        return jnp.sum(jnp.where(eye, jnp.broadcast_to(col, (block, block)), 0.0), axis=0)[None]

    cols = []
    for b in range(blocks):
        cols.append(jnp.sum(jnp.where(lane <= row + b * block, step, 0.0), axis=1, keepdims=True))
    rows = [to_row(col, b * block) for b, col in enumerate(cols)]
    first = jnp.zeros((1, LANES), F32)
    last = jnp.zeros((1, LANES), F32)
    for b in range(blocks):
        first = jnp.where(edge == blocks + b, rows[b][:, :1], first)
        last = jnp.where(edge == b, rows[b][:, -1:], last)
    for b in range(blocks):
        near = dot_free_spread(cols[b], edge, blocks, b, first, last)
        spread_ref[b * block : (b + 1) * block, :] = near.astype(BF16)
        inside = along_gain * jnp.exp(-jnp.abs(cols[b] - rows[b]))
        block_ref[:block, b * block : (b + 1) * block] = inside.astype(BF16)
        which = lax.broadcasted_iota(jnp.int32, (LANES, block), 0)
        enter = jnp.zeros((LANES, block), F32)
        for a in range(blocks):
            if a < b:
                reach = rows[b] - rows[a][:, -1:]
                enter = jnp.where(which == a, jnp.exp(-reach), enter)
            if a > b:
                reach = rows[a][:, :1] - rows[b]
                enter = jnp.where(which == blocks + a, jnp.exp(-reach), enter)
        block_ref[block:, b * block : (b + 1) * block] = (along_gain * enter).astype(BF16)


def dot_free_spread(col, edge, blocks, b, first, last):
    to_last = jnp.exp(jnp.minimum(col - last, 0.0))
    to_first = jnp.exp(jnp.minimum(first - col, 0.0))
    return jnp.where(edge == b, to_last, 0.0) + jnp.where(edge == blocks + b, to_first, 0.0)


def prepare_x(step_x, block, after):
    columns = step_x.shape[0]
    return pl.pallas_call(
        functools.partial(prepare_x_kernel, block),
        in_specs=[pl.BlockSpec(memory_space=pltpu.VMEM), pl.BlockSpec(memory_space=pl.ANY)],
        out_shape=(
            jax.ShapeDtypeStruct((columns, LANES), BF16),
            jax.ShapeDtypeStruct((block + LANES, columns), BF16),
        ),
        compiler_params=params(),
        cost_estimate=cost(20 * columns * columns, 2 * columns * block),
        name="prepare_x",
    )(step_x[None], after)


def prepare_y_kernel(levels, tile_ref, step_y_ref, step_z_ref, after_ref, mix_ref, halo_ref, token_ref):
    size = mix_ref.shape[0]
    rows = size // levels
    base = tile_ref[0] * rows

    def split(shape, axis):
        index = lax.broadcasted_iota(jnp.int32, shape, axis)
        level = ((index.astype(F32) + 0.5) * (1.0 / rows)).astype(jnp.int32)
        return index, level, index - level * rows

    def coordinate(step_ref, upto):
        step = step_ref[...]
        shape = (upto.shape[0], step.shape[1])
        lane = lax.broadcasted_iota(jnp.int32, shape, 1)
        return jnp.sum(jnp.where(lane <= upto, jnp.broadcast_to(step, shape), 0.0), axis=1, keepdims=True)

    _, out_level, out_row = split((size, 1), 0)
    out_y = coordinate(step_y_ref, out_row + base)
    out_z = coordinate(step_z_ref, out_level)
    eye = lax.broadcasted_iota(jnp.int32, (size, size), 0) == lax.broadcasted_iota(
        jnp.int32, (size, size), 1
    )

    def to_row(col):
        return jnp.sum(jnp.where(eye, jnp.broadcast_to(col, (size, size)), 0.0), axis=0, keepdims=True)

    in_y = to_row(out_y)
    in_z = to_row(out_z)
    _, in_level, _ = split((1, size), 1)
    distance = jnp.abs(out_y - in_y) + jnp.abs(out_z - in_z)
    value = (horiz_gain * vert_gain) * jnp.exp(-distance)
    mix_ref[...] = jnp.where(jnp.abs(out_level - in_level) <= BAND, value, 0.0).astype(BF16)

    wide = 2 * levels
    column = lax.broadcasted_iota(jnp.int32, (1, wide), 1)
    halo_level = jnp.where(column < levels, column, column - levels)
    step_y = step_y_ref[...]
    lane = lax.broadcasted_iota(jnp.int32, step_y.shape, 1)
    below = jnp.sum(jnp.where(lane <= base - 1, step_y, 0.0), axis=1, keepdims=True)
    above = jnp.sum(jnp.where(lane <= base + rows, step_y, 0.0), axis=1, keepdims=True)
    step_z = step_z_ref[...]
    order = lax.broadcasted_iota(jnp.int32, (step_z.shape[1], wide), 0)
    turned = lax.broadcasted_iota(jnp.int32, (step_z.shape[1], step_z.shape[1]), 0)
    turned = turned == lax.broadcasted_iota(jnp.int32, turned.shape, 1)
    step_col = jnp.sum(jnp.where(turned, jnp.broadcast_to(step_z, turned.shape), 0.0), axis=1, keepdims=True)
    halo_z = jnp.sum(jnp.where(order <= halo_level, jnp.broadcast_to(step_col, order.shape), 0.0), axis=0, keepdims=True)
    reach = jnp.where(column < levels, out_y - below, above - out_y)
    value = (horiz_gain * vert_gain) * jnp.exp(-(jnp.abs(reach) + jnp.abs(out_z - halo_z)))
    halo_ref[...] = jnp.where(jnp.abs(out_level - halo_level) <= BAND, value, 0.0).astype(BF16)
    token_ref[...] = jnp.zeros_like(token_ref)


def prepare_y(tile, step_y, step_z, levels, size, after):
    return pl.pallas_call(
        functools.partial(prepare_y_kernel, levels),
        grid_spec=pltpu.PrefetchScalarGridSpec(
            num_scalar_prefetch=1,
            grid=(1,),
            in_specs=[
                pl.BlockSpec((1, step_y.shape[0]), lambda i, t: (0, 0)),
                pl.BlockSpec((1, step_z.shape[0]), lambda i, t: (0, 0)),
                pl.BlockSpec(memory_space=pl.ANY),
            ],
            out_specs=[
                pl.BlockSpec((size, size), lambda i, t: (0, 0)),
                pl.BlockSpec((size, 2 * levels), lambda i, t: (0, 0)),
                pl.BlockSpec((1, 2), lambda i, t: (0, 0)),
            ],
        ),
        out_shape=[
            jax.ShapeDtypeStruct((size, size), BF16),
            jax.ShapeDtypeStruct((size, 2 * levels), BF16),
            jax.ShapeDtypeStruct((1, 2), F32),
        ],
        compiler_params=params(),
        cost_estimate=cost(20 * size * size, size * size),
        name="prepare_y",
    )(tile[None], step_y[None], step_z[None], after)


def edge_kernel(levels, rows, tile_ref, step_ref, field_ref, edge_ref, out_ref):
    @pl.when(jnp.logical_and(pl.program_id(0) == 0, pl.program_id(1) == 0))
    def _():
        base = tile_ref[0] * rows
        steps = step_ref.shape[1]
        size = edge_ref.shape[1]
        at = lax.broadcasted_iota(jnp.int32, (rows, steps), 1) - base
        row = lax.broadcasted_iota(jnp.int32, (rows, steps), 0)
        step = jnp.broadcast_to(step_ref[...], (rows, steps))
        own = jnp.sum(jnp.where(jnp.logical_and(at == row, row > 0), step, 0.0), axis=1, keepdims=True)
        column = lax.broadcasted_iota(jnp.int32, (1, size), 1)
        level = ((column.astype(F32) + 0.5) * (1.0 / rows)).astype(jnp.int32)
        row = lax.broadcasted_iota(jnp.int32, (rows, size), 0)
        reached = jnp.where(row <= column - level * rows, jnp.broadcast_to(own, (rows, size)), 0.0)
        from_first = jnp.sum(reached, axis=0, keepdims=True)
        to_last = jnp.sum(own, axis=0, keepdims=True) - from_first
        which = lax.broadcasted_iota(jnp.int32, (2 * levels, 1), 0)
        ending = which < levels
        reach = jnp.where(ending, to_last, from_first)
        own_level = jnp.where(ending, which, which - levels) == level
        edge_ref[...] = jnp.where(own_level, jnp.exp(-jnp.abs(reach)), 0.0).astype(BF16)

    out_ref[...] = dot(edge_ref[...], field_ref[...]).astype(BF16)


def edge_sums(tile, step_y, levels, field):
    count, size, columns = field.shape
    block = pick_block(columns, 768, 256, 128)
    return pl.pallas_call(
        functools.partial(edge_kernel, levels, size // levels),
        grid_spec=pltpu.PrefetchScalarGridSpec(
            num_scalar_prefetch=1,
            grid=(count, columns // block),
            in_specs=[
                pl.BlockSpec((1, step_y.shape[0]), lambda m, j, t: (0, 0)),
                pl.BlockSpec((None, size, block), lambda m, j, t: (m, 0, j)),
            ],
            out_specs=[
                pl.BlockSpec((2 * levels, size), lambda m, j, t: (0, 0)),
                pl.BlockSpec((None, 2 * levels, block), lambda m, j, t: (m, 0, j)),
            ],
        ),
        out_shape=[
            jax.ShapeDtypeStruct((2 * levels, size), BF16),
            jax.ShapeDtypeStruct((count, 2 * levels, columns), BF16),
        ],
        compiler_params=params(),
        cost_estimate=cost(4 * levels * field.size, field.size),
        name="edge_sums",
    )(tile[None], step_y[None], field)


def weigh_kernel(edge_ref, memb_ref, grad_ref, after_ref, out_ref):
    out_ref[...] = dot(edge_ref[...], memb_ref[...] * grad_ref[...]).astype(BF16)


def weighted_edge_sums(which, edge, memb, grad, after):
    count, rows, columns = memb.shape
    half = columns // 2
    block = pick_block(half, 384, 256, 128)
    steps = half // block
    return pl.pallas_call(
        weigh_kernel,
        grid=(steps, count),
        in_specs=[
            pl.BlockSpec(edge.shape, lambda j, m: (0, 0)),
            pl.BlockSpec((None, rows, block), lambda j, m: (m, 0, which * steps + j)),
            pl.BlockSpec((rows, block), lambda j, m: (0, j)),
            pl.BlockSpec(memory_space=pl.ANY),
        ],
        out_specs=pl.BlockSpec((None, edge.shape[0], block), lambda j, m: (m, 0, j)),
        out_shape=jax.ShapeDtypeStruct((count, edge.shape[0], half), BF16),
        compiler_params=params(),
        cost_estimate=cost(edge.shape[0] * memb.size, memb.size),
        name="weighted_edge_sums",
    )(edge, memb, grad, after)


def filter_x_kernel(block, count, field_ref, *refs):
    weights, (spread_ref, block_ref), (out_ref, token_ref) = refs[:count], refs[count : count + 2], refs[-2:]
    field = field_ref[...]
    if weights:
        field = field * jnp.concatenate([ref[...] for ref in weights], axis=1)
    edges = dot(field, spread_ref[...]).astype(BF16)
    for start in range(0, field.shape[1], block):
        part = slice(start, start + block)
        both = jnp.concatenate([field[:, part], edges], axis=1)
        out_ref[:, part] = dot(both, block_ref[:, part]).astype(BF16)
    token_ref[...] = jnp.zeros_like(token_ref)


def filter_x(members, field, weights, spread_x, block_x, after):
    count, rows, columns = field.shape
    height = pick_block(rows, 384, 256, 128)
    block = block_x.shape[0] - LANES
    whole = lambda i, m: (0, 0)
    return pl.pallas_call(
        functools.partial(filter_x_kernel, block, len(weights)),
        grid=(rows // height, len(members)),
        in_specs=[
            pl.BlockSpec((None, height, columns), lambda i, m: (members[0] + m, i, 0)),
            *[pl.BlockSpec((height, columns // 2), lambda i, m: (i, 0)) for _ in weights],
            pl.BlockSpec(spread_x.shape, whole),
            pl.BlockSpec(block_x.shape, whole),
            *[pl.BlockSpec(memory_space=pl.ANY) for _ in after],
        ],
        out_specs=[
            pl.BlockSpec((None, height, columns), lambda i, m: (m, i, 0)),
            pl.BlockSpec((1, 2), whole),
        ],
        out_shape=[
            jax.ShapeDtypeStruct((len(members), rows, columns), BF16),
            jax.ShapeDtypeStruct((1, 2), F32),
        ],
        compiler_params=params(),
        cost_estimate=cost(
            2 * len(members) * rows * columns * (block + 2 * LANES), 2 * len(members) * rows * columns
        ),
        name="filter_x",
    )(field, *weights, spread_x, block_x, *after)


def halo_along_x(at, halo, sums, block_ref, block):
    part = halo[:, pl.ds(pl.multiple_of(at * block, block), block)]
    return dot(jnp.concatenate([part, sums], axis=1), block_ref[...]).astype(BF16)


def increment_kernel(
    block, first_ref, mix_ref, mix_halo_ref, memb_ref, halo_ref, spread_ref, block_ref, *refs
):
    count = memb_ref.shape[0]
    fields, out_ref, sums_ref = refs[:count], refs[-2], refs[-1]
    step = pl.program_id(0)

    @pl.when(step == 0)
    def _():
        for m in range(count):
            sums_ref[m] = dot(halo_ref[m], spread_ref[...]).astype(BF16)

    total = None
    for m in range(count):
        halo = halo_along_x(first_ref[0] + step, halo_ref.at[m], sums_ref[m], block_ref, block)
        shaped = dot(mix_ref[...], fields[m][...]) + dot(mix_halo_ref[...], halo)
        term = shaped * memb_ref[m].astype(F32)
        total = term if total is None else total + term
    out_ref[...] = total.astype(BF16)


def partial_increment(first, after, blocks, mix, mix_halo, fields, memb, halo, spread_x, block_x):
    count, rows, columns = memb.shape
    block = block_x.shape[0] - LANES
    pick = lambda j, first: (0, 0, first[0] + j)
    whole2 = lambda j, first: (0, 0)
    return pl.pallas_call(
        functools.partial(increment_kernel, block),
        grid_spec=pltpu.PrefetchScalarGridSpec(
            num_scalar_prefetch=1,
            grid=(blocks,),
            in_specs=[
                pl.BlockSpec(mix.shape, whole2),
                pl.BlockSpec(mix_halo.shape, whole2),
                pl.BlockSpec((count, rows, block), pick),
                pl.BlockSpec(halo.shape, lambda j, first: (0, 0, 0)),
                pl.BlockSpec(spread_x.shape, whole2),
                pl.BlockSpec((block_x.shape[0], block), lambda j, first: (0, first[0] + j)),
                *[pl.BlockSpec((None, rows, block), pick) for _ in fields],
                pl.BlockSpec(memory_space=pl.ANY),
            ],
            out_specs=pl.BlockSpec((rows, block), lambda j, first: (0, j)),
            scratch_shapes=[pltpu.VMEM((count, halo.shape[1], LANES), BF16)],
        ),
        out_shape=jax.ShapeDtypeStruct((rows, blocks * block), BF16),
        compiler_params=params(),
        cost_estimate=cost(
            2 * count * rows * (rows + halo.shape[1]) * blocks * block,
            2 * count * rows * blocks * block + rows * rows,
        ),
        name="partial_increment",
    )(first[None], mix, mix_halo, memb, halo, spread_x, block_x, *fields, after)


def join_kernel(own_ref, other_ref, after_ref, out_ref):
    out_ref[...] = (own_ref[...].astype(F32) + other_ref[...].astype(F32)).astype(BF16)


def join(own, other, after):
    rows, columns = own.shape
    height = pick_block(rows, 384, 256, 128)
    block = pl.BlockSpec((height, columns), lambda i: (i, 0))
    return pl.pallas_call(
        join_kernel,
        grid=(rows // height,),
        in_specs=[block, block, pl.BlockSpec(memory_space=pl.ANY)],
        out_specs=block,
        out_shape=jax.ShapeDtypeStruct(own.shape, BF16),
        compiler_params=params(),
        cost_estimate=cost(own.size, 3 * own.size),
        name="join",
    )(own, other, after)


def zero_kernel(*refs):
    refs[-1][...] = jnp.zeros_like(refs[-1])


def zero_after(*after):
    return pl.pallas_call(
        zero_kernel,
        in_specs=[pl.BlockSpec(memory_space=pl.ANY)] * len(after),
        out_shape=jax.ShapeDtypeStruct((1, 2), F32),
        name="zero_after",
    )(*after)


def hold_kernel(*refs):
    del refs


def hold(array, *after):
    return pl.pallas_call(
        hold_kernel,
        in_specs=[pl.BlockSpec(memory_space=pl.ANY)] * (1 + len(after)),
        out_specs=pl.BlockSpec(memory_space=pl.ANY),
        out_shape=jax.ShapeDtypeStruct(array.shape, array.dtype),
        input_output_aliases={0: 0},
        name="hold",
    )(array, *after)


def adjoint_inside_kernel(mix_ref, memb_ref, grad_ref, after_ref, out_ref):
    out_ref[...] = dot(mix_ref[...], memb_ref[...] * grad_ref[...]).astype(BF16)


def adjoint_inside(which, mix, memb, grad, after):
    count, rows, columns = memb.shape
    half = columns // 2
    block = pick_block(half, 384, 256, 128)
    steps = half // block
    return pl.pallas_call(
        adjoint_inside_kernel,
        grid=(steps, count),
        in_specs=[
            pl.BlockSpec(mix.shape, lambda j, m: (0, 0)),
            pl.BlockSpec((None, rows, block), lambda j, m: (m, 0, which * steps + j)),
            pl.BlockSpec((rows, block), lambda j, m: (0, j)),
            pl.BlockSpec(memory_space=pl.ANY),
        ],
        out_specs=pl.BlockSpec((None, rows, block), lambda j, m: (m, 0, j)),
        out_shape=jax.ShapeDtypeStruct((count, rows, half), BF16),
        compiler_params=params(),
        cost_estimate=cost(rows * memb.size, memb.size + rows * rows),
        name="adjoint_inside",
    )(mix, memb, grad, after)


def adjoint_kernel(
    block, left_ref, right_ref, mix_halo_ref, halo_ref, spread_ref, block_ref, out_ref
):
    inside = jnp.concatenate([left_ref[...], right_ref[...]], axis=1)
    field = (dot(mix_halo_ref[...], halo_ref[...]) + inside.astype(F32)).astype(BF16)
    edges = dot(field, spread_ref[...]).astype(BF16)
    for start in range(0, field.shape[1], block):
        part = slice(start, start + block)
        both = jnp.concatenate([field[:, part], edges], axis=1)
        out_ref[:, part] = dot(both, block_ref[:, part]).astype(BF16)


def adjoint_outside(left, right, mix_halo, halo, spread_x, block_x):
    count, rows, half = left.shape
    height = pick_block(rows, 384, 256, 128)
    block = block_x.shape[0] - LANES
    pick = lambda m, i: (m, i, 0)
    whole = lambda m, i: (0, 0)
    return pl.pallas_call(
        functools.partial(adjoint_kernel, block),
        grid=(count, rows // height),
        in_specs=[
            pl.BlockSpec((None, height, half), pick),
            pl.BlockSpec((None, height, half), pick),
            pl.BlockSpec((height, mix_halo.shape[1]), lambda m, i: (i, 0)),
            pl.BlockSpec((None,) + halo.shape[1:], lambda m, i: (m, 0, 0)),
            pl.BlockSpec(spread_x.shape, whole),
            pl.BlockSpec(block_x.shape, whole),
        ],
        out_specs=pl.BlockSpec((None, height, 2 * half), pick),
        out_shape=jax.ShapeDtypeStruct((count, rows, 2 * half), BF16),
        compiler_params=params(),
        cost_estimate=cost(4 * left.size * (block + 2 * LANES), 4 * left.size),
        name="adjoint_outside",
    )(left, right, mix_halo, halo, spread_x, block_x)


def hop_factors(tile, tiles, rows, step_y):
    hops = np.array([1 << k for k in range(tiles.bit_length() - 1)], np.int32)
    pair = tile - lax.rem(tile, 2)
    group = tile - lax.rem(jnp.broadcast_to(tile, hops.shape), hops)
    upper = lax.rem(lax.div(group, hops), np.int32(2)) == 1
    first = jnp.where(upper, group - hops, group)
    middle = first + hops
    base = jnp.where(hops == 1, tile, pair)
    after = jnp.where(hops == 1, tile + 1, pair + 2)
    frm = [middle * rows - 1, first * rows, middle * rows - 1, after * rows]
    to = [(middle + hops) * rows - 1, middle * rows, base * rows - 1, middle * rows]
    frm = jnp.concatenate(frm + [jnp.stack([pair * rows - 1, (tile + 1) * rows])])
    to = jnp.concatenate(to + [jnp.stack([tile * rows - 1, (pair + 2) * rows])])
    index = jnp.arange(step_y.shape[0], dtype=jnp.int32)[None]
    between = jnp.logical_and(index > frm[:, None], index <= to[:, None])
    factor = jnp.exp(-jnp.sum(jnp.where(between, step_y[None], 0.0), axis=1))
    end, start, below, above = [factor[k * len(hops) : (k + 1) * len(hops)] for k in range(4)]
    upper = upper.astype(F32)
    lower = 1.0 - upper
    ways = [
        upper + lower * end, upper * start + lower,
        upper * end + lower, upper + lower * start,
        upper * below, lower * above,
    ]
    return jnp.stack(ways, axis=1).reshape(len(hops), 3, 2), factor[4 * len(hops) :]


def outside(sums, tile, tiles, levels, factors, meanwhile):
    count, _, columns = sums.shape
    sums = sums.reshape(count, 2, levels, columns)
    part = count // 2
    odd = lax.rem(tile, 2)
    factor, way = factors

    def pair(x, hop):
        return lax.ppermute(x, "tile", [(s, s ^ hop) for s in range(tiles)])

    def by_way(pair_of):
        return pair_of.reshape(1, 2, 1, 1)

    other = pair(sums, 1)
    mine = lax.dynamic_slice_in_dim(sums, odd * part, part, 0).astype(F32)
    theirs = lax.dynamic_slice_in_dim(other, odd * part, part, 0).astype(F32)
    group = (by_way(factor[0, 0]) * mine + by_way(factor[0, 1]) * theirs).astype(BF16)
    token = meanwhile(0, other)
    far = jnp.zeros(group.shape, F32)
    hop, at = 2, 1
    while hop < tiles:
        enter = factor[at, 2]
        if 2 * hop < tiles:
            theirs = pair(group, hop)
            came = theirs
            keep = factor[at, 0]
            if token is not None:
                keep = keep + token[0]
            group = by_way(keep) * group.astype(F32) + by_way(factor[at, 1]) * theirs.astype(F32)
            group = group.astype(BF16)
        else:
            upper = lax.rem(lax.div(tile, hop), 2) == 1
            theirs = pair(jnp.where(upper, group[:, 1], group[:, 0]), hop)
            came = theirs[:, None]
            if token is not None:
                enter = enter + token[0]
        far += by_way(enter) * came.astype(F32)
        token = meanwhile(at, theirs)
        hop *= 2
        at += 1
    far = far.astype(BF16)
    there = pair(far, 1)
    far = jnp.where(
        odd == 0,
        jnp.concatenate([far, there], axis=0),
        jnp.concatenate([there, far], axis=0),
    )
    halo = far.astype(F32) * by_way(way) + other.astype(F32) * by_way(factor[0, 2])
    return halo.astype(BF16).reshape(count, 2 * levels, columns), theirs


def body(tiles, control, members, gradient, step_x, step_y, step_z):
    count, levels, rows, columns = control.shape
    flat = (count, levels * rows, columns)
    tile = lax.axis_index("tile")
    side = lax.axis_index("mem")
    half = columns // 2
    block = pick_block(half, 256, 128)
    owned = gradient.shape[0]
    def in_order(own, other, axis):
        return jnp.where(
            side == 0,
            jnp.concatenate([own, other], axis=axis),
            jnp.concatenate([other, own], axis=axis),
        )

    def to_rows(part):
        part = part.reshape(owned, tiles, rows, -1).swapaxes(0, 1).reshape(levels, rows, -1)
        return lax.all_to_all(part, "tile", 0, 0, tiled=True).reshape(levels * rows, -1)

    def to_levels(part):
        part = lax.all_to_all(part.reshape(levels, rows, -1), "tile", 0, 0, tiled=True)
        part = part.reshape(tiles, owned, rows, -1).swapaxes(0, 1)
        return part.reshape(owned, tiles * rows, -1)

    left = to_rows(gradient[:, :, :half])

    factors = hop_factors(tile, tiles, rows, step_y)
    field = control.reshape(flat)
    memb = members.reshape(flat)
    edge, control_sums = edge_sums(tile, step_y, levels, field)
    along, mixes, factors_x = [], [], []

    def prepare(k, came):
        if k == 0:
            factors_x.extend(prepare_x(step_x, block, came))
        if k < count:
            result, token = filter_x([k], field, (), *factors_x, (came,))
            along.append(result)
            return token
        if k == count:
            *result, token = prepare_y(tile, step_y, step_z, levels, levels * rows, came)
            mixes.extend(result)
            return token
        return None

    halo, last = outside(control_sums, tile, tiles, levels, factors, prepare)
    for k in range(len(along) + len(mixes) // 2, count + 1):
        prepare(k, last)
    mix, mix_halo = mixes
    spread_x, block_x = factors_x

    right = to_rows(hold(gradient[:, :, half:], last, mix))

    blocks = half // block
    sizes = CHUNKS if sum(CHUNKS) == blocks else [blocks]
    starts = [sum(sizes[:k]) for k in range(len(sizes))]
    share = functools.partial(
        partial_increment,
        mix=mix, mix_halo=mix_halo, fields=along, memb=memb, halo=halo, spread_x=spread_x,
        block_x=block_x,
    )
    sent, now = [], halo
    for at, size in zip(starts, sizes):
        now = share((1 - side) * blocks + at, now, blocks=size)
        sent.append(now)
    others = [lax.ppermute(x, "mem", SWAP) for x in sent]
    now = left_sums = weighted_edge_sums(0, edge, memb, left, now)
    mine, rest = [], []
    for k, (at, size) in enumerate(zip(starts, sizes)):
        now = own = share(side * blocks + at, now, blocks=size)
        if k == 0:
            now = right_sums = weighted_edge_sums(1, edge, memb, right, now)
        if k == len(sizes) - 1:
            now = left_inside = adjoint_inside(0, mix, memb, left, now)
        now = join(own, others[k], now)
        mine.append(to_levels(now))
        rest.append(lax.ppermute(mine[-1], "mem", SWAP))
    increment = in_order(jnp.concatenate(mine, axis=2), jnp.concatenate(rest, axis=2), 2)

    right_inside = adjoint_inside(1, mix, memb, right, now)
    hops = tiles.bit_length() - 1

    def wait(k, came):
        return zero_after(came, mine[0], right_inside) if k == hops - 3 else None

    weighted_sums = jnp.concatenate([left_sums, right_sums], axis=2)
    weighted_halo, _ = outside(weighted_sums, tile, tiles, levels, factors, wait)
    control_grad = adjoint_outside(
        left_inside, right_inside, mix_halo, weighted_halo, spread_x, block_x
    )
    return increment, control_grad.reshape(control.shape)


def solution(mesh):
    placed = (
        P("mem", None, "tile", None),
        P("mem", None, "tile", None),
        P("tile", None, None),
        P(),
        P(),
        P(),
    )
    return jax.shard_map(
        functools.partial(body, mesh.shape["tile"]),
        mesh=mesh,
        in_specs=placed,
        out_specs=(P("tile", None, None), P("mem", None, "tile", None)),
        check_vma=False,
    )
```

```python
import functools

import jax
import jax.numpy as jnp
import numpy as np
from jax import lax
from jax.experimental import pallas as pl
from jax.experimental.pallas import tpu as pltpu
from jax.sharding import PartitionSpec as P

BAND = 8

along_gain = 0.35
horiz_gain = 0.15
vert_gain = 0.5

BF16 = jnp.bfloat16
F32 = jnp.float32
VMEM_LIMIT = 60 * 1024 * 1024
LANES = 128
SWAP = [(0, 1), (1, 0)]
CHUNKS = [2, 1]


def params():
    return pltpu.CompilerParams(vmem_limit_bytes=VMEM_LIMIT)


def cost(flops, values):
    return pl.CostEstimate(flops=flops, bytes_accessed=2 * values, transcendentals=0)


def pick_block(size, *wanted):
    for block in wanted:
        if size % block == 0:
            return block
    return size


def dot(a, b):
    return jnp.dot(a, b, preferred_element_type=F32)


def prepare_x_kernel(block, step_ref, after_ref, spread_ref, block_ref):
    columns = step_ref.shape[1]
    blocks = columns // block
    step = jnp.broadcast_to(step_ref[...], (block, columns))
    lane = lax.broadcasted_iota(jnp.int32, (block, columns), 1)
    row = lax.broadcasted_iota(jnp.int32, (block, columns), 0)
    edge = lax.broadcasted_iota(jnp.int32, (1, LANES), 1)
    firsts = jnp.where(edge < blocks, edge, edge - blocks) * block

    def to_row(col, first):
        eye = lax.broadcasted_iota(jnp.int32, (block, block), 0) == lax.broadcasted_iota(
            jnp.int32, (block, block), 1
        )
        return jnp.sum(jnp.where(eye, jnp.broadcast_to(col, (block, block)), 0.0), axis=0)[None]

    cols = []
    for b in range(blocks):
        cols.append(jnp.sum(jnp.where(lane <= row + b * block, step, 0.0), axis=1, keepdims=True))
    rows = [to_row(col, b * block) for b, col in enumerate(cols)]
    first = jnp.zeros((1, LANES), F32)
    last = jnp.zeros((1, LANES), F32)
    for b in range(blocks):
        first = jnp.where(edge == blocks + b, rows[b][:, :1], first)
        last = jnp.where(edge == b, rows[b][:, -1:], last)
    for b in range(blocks):
        near = dot_free_spread(cols[b], edge, blocks, b, first, last)
        spread_ref[b * block : (b + 1) * block, :] = near.astype(BF16)
        inside = along_gain * jnp.exp(-jnp.abs(cols[b] - rows[b]))
        block_ref[:block, b * block : (b + 1) * block] = inside.astype(BF16)
        which = lax.broadcasted_iota(jnp.int32, (LANES, block), 0)
        enter = jnp.zeros((LANES, block), F32)
        for a in range(blocks):
            if a < b:
                reach = rows[b] - rows[a][:, -1:]
                enter = jnp.where(which == a, jnp.exp(-reach), enter)
            if a > b:
                reach = rows[a][:, :1] - rows[b]
                enter = jnp.where(which == blocks + a, jnp.exp(-reach), enter)
        block_ref[block:, b * block : (b + 1) * block] = (along_gain * enter).astype(BF16)


def dot_free_spread(col, edge, blocks, b, first, last):
    to_last = jnp.exp(jnp.minimum(col - last, 0.0))
    to_first = jnp.exp(jnp.minimum(first - col, 0.0))
    return jnp.where(edge == b, to_last, 0.0) + jnp.where(edge == blocks + b, to_first, 0.0)


def prepare_x(step_x, block, after):
    columns = step_x.shape[0]
    return pl.pallas_call(
        functools.partial(prepare_x_kernel, block),
        in_specs=[pl.BlockSpec(memory_space=pltpu.VMEM), pl.BlockSpec(memory_space=pl.ANY)],
        out_shape=(
            jax.ShapeDtypeStruct((columns, LANES), BF16),
            jax.ShapeDtypeStruct((block + LANES, columns), BF16),
        ),
        compiler_params=params(),
        cost_estimate=cost(20 * columns * columns, 2 * columns * block),
        name="prepare_x",
    )(step_x[None], after)


def prepare_y_kernel(levels, tile_ref, step_y_ref, step_z_ref, after_ref, mix_ref, halo_ref, token_ref):
    size = mix_ref.shape[0]
    rows = size // levels
    base = tile_ref[0] * rows

    def split(shape, axis):
        index = lax.broadcasted_iota(jnp.int32, shape, axis)
        level = ((index.astype(F32) + 0.5) * (1.0 / rows)).astype(jnp.int32)
        return index, level, index - level * rows

    def coordinate(step_ref, upto):
        step = step_ref[...]
        shape = (upto.shape[0], step.shape[1])
        lane = lax.broadcasted_iota(jnp.int32, shape, 1)
        return jnp.sum(jnp.where(lane <= upto, jnp.broadcast_to(step, shape), 0.0), axis=1, keepdims=True)

    _, out_level, out_row = split((size, 1), 0)
    out_y = coordinate(step_y_ref, out_row + base)
    out_z = coordinate(step_z_ref, out_level)
    eye = lax.broadcasted_iota(jnp.int32, (size, size), 0) == lax.broadcasted_iota(
        jnp.int32, (size, size), 1
    )

    def to_row(col):
        return jnp.sum(jnp.where(eye, jnp.broadcast_to(col, (size, size)), 0.0), axis=0, keepdims=True)

    in_y = to_row(out_y)
    in_z = to_row(out_z)
    _, in_level, _ = split((1, size), 1)
    distance = jnp.abs(out_y - in_y) + jnp.abs(out_z - in_z)
    value = (horiz_gain * vert_gain) * jnp.exp(-distance)
    mix_ref[...] = jnp.where(jnp.abs(out_level - in_level) <= BAND, value, 0.0).astype(BF16)

    wide = 2 * levels
    column = lax.broadcasted_iota(jnp.int32, (1, wide), 1)
    halo_level = jnp.where(column < levels, column, column - levels)
    step_y = step_y_ref[...]
    lane = lax.broadcasted_iota(jnp.int32, step_y.shape, 1)
    below = jnp.sum(jnp.where(lane <= base - 1, step_y, 0.0), axis=1, keepdims=True)
    above = jnp.sum(jnp.where(lane <= base + rows, step_y, 0.0), axis=1, keepdims=True)
    step_z = step_z_ref[...]
    order = lax.broadcasted_iota(jnp.int32, (step_z.shape[1], wide), 0)
    turned = lax.broadcasted_iota(jnp.int32, (step_z.shape[1], step_z.shape[1]), 0)
    turned = turned == lax.broadcasted_iota(jnp.int32, turned.shape, 1)
    step_col = jnp.sum(jnp.where(turned, jnp.broadcast_to(step_z, turned.shape), 0.0), axis=1, keepdims=True)
    halo_z = jnp.sum(jnp.where(order <= halo_level, jnp.broadcast_to(step_col, order.shape), 0.0), axis=0, keepdims=True)
    reach = jnp.where(column < levels, out_y - below, above - out_y)
    value = (horiz_gain * vert_gain) * jnp.exp(-(jnp.abs(reach) + jnp.abs(out_z - halo_z)))
    halo_ref[...] = jnp.where(jnp.abs(out_level - halo_level) <= BAND, value, 0.0).astype(BF16)
    token_ref[...] = jnp.zeros_like(token_ref)


def prepare_y(tile, step_y, step_z, levels, size, after):
    return pl.pallas_call(
        functools.partial(prepare_y_kernel, levels),
        grid_spec=pltpu.PrefetchScalarGridSpec(
            num_scalar_prefetch=1,
            grid=(1,),
            in_specs=[
                pl.BlockSpec((1, step_y.shape[0]), lambda i, t: (0, 0)),
                pl.BlockSpec((1, step_z.shape[0]), lambda i, t: (0, 0)),
                pl.BlockSpec(memory_space=pl.ANY),
            ],
            out_specs=[
                pl.BlockSpec((size, size), lambda i, t: (0, 0)),
                pl.BlockSpec((size, 2 * levels), lambda i, t: (0, 0)),
                pl.BlockSpec((1, 2), lambda i, t: (0, 0)),
            ],
        ),
        out_shape=[
            jax.ShapeDtypeStruct((size, size), BF16),
            jax.ShapeDtypeStruct((size, 2 * levels), BF16),
            jax.ShapeDtypeStruct((1, 2), F32),
        ],
        compiler_params=params(),
        cost_estimate=cost(20 * size * size, size * size),
        name="prepare_y",
    )(tile[None], step_y[None], step_z[None], after)


def edge_kernel(levels, rows, tile_ref, step_ref, field_ref, edge_ref, out_ref):
    @pl.when(jnp.logical_and(pl.program_id(0) == 0, pl.program_id(1) == 0))
    def _():
        base = tile_ref[0] * rows
        steps = step_ref.shape[1]
        size = edge_ref.shape[1]
        at = lax.broadcasted_iota(jnp.int32, (rows, steps), 1) - base
        row = lax.broadcasted_iota(jnp.int32, (rows, steps), 0)
        step = jnp.broadcast_to(step_ref[...], (rows, steps))
        own = jnp.sum(jnp.where(jnp.logical_and(at == row, row > 0), step, 0.0), axis=1, keepdims=True)
        column = lax.broadcasted_iota(jnp.int32, (1, size), 1)
        level = ((column.astype(F32) + 0.5) * (1.0 / rows)).astype(jnp.int32)
        row = lax.broadcasted_iota(jnp.int32, (rows, size), 0)
        reached = jnp.where(row <= column - level * rows, jnp.broadcast_to(own, (rows, size)), 0.0)
        from_first = jnp.sum(reached, axis=0, keepdims=True)
        to_last = jnp.sum(own, axis=0, keepdims=True) - from_first
        which = lax.broadcasted_iota(jnp.int32, (2 * levels, 1), 0)
        ending = which < levels
        reach = jnp.where(ending, to_last, from_first)
        own_level = jnp.where(ending, which, which - levels) == level
        edge_ref[...] = jnp.where(own_level, jnp.exp(-jnp.abs(reach)), 0.0).astype(BF16)

    out_ref[...] = dot(edge_ref[...], field_ref[...]).astype(BF16)


def edge_sums(tile, step_y, levels, field):
    count, size, columns = field.shape
    block = pick_block(columns, 768, 256, 128)
    return pl.pallas_call(
        functools.partial(edge_kernel, levels, size // levels),
        grid_spec=pltpu.PrefetchScalarGridSpec(
            num_scalar_prefetch=1,
            grid=(count, columns // block),
            in_specs=[
                pl.BlockSpec((1, step_y.shape[0]), lambda m, j, t: (0, 0)),
                pl.BlockSpec((None, size, block), lambda m, j, t: (m, 0, j)),
            ],
            out_specs=[
                pl.BlockSpec((2 * levels, size), lambda m, j, t: (0, 0)),
                pl.BlockSpec((None, 2 * levels, block), lambda m, j, t: (m, 0, j)),
            ],
        ),
        out_shape=[
            jax.ShapeDtypeStruct((2 * levels, size), BF16),
            jax.ShapeDtypeStruct((count, 2 * levels, columns), BF16),
        ],
        compiler_params=params(),
        cost_estimate=cost(4 * levels * field.size, field.size),
        name="edge_sums",
    )(tile[None], step_y[None], field)


def weigh_kernel(edge_ref, memb_ref, grad_ref, after_ref, out_ref):
    out_ref[...] = dot(edge_ref[...], memb_ref[...] * grad_ref[...]).astype(BF16)


def weighted_edge_sums(which, edge, memb, grad, after):
    count, rows, columns = memb.shape
    half = columns // 2
    block = pick_block(half, 768, 256, 128)
    steps = half // block
    return pl.pallas_call(
        weigh_kernel,
        grid=(steps, count),
        in_specs=[
            pl.BlockSpec(edge.shape, lambda j, m: (0, 0)),
            pl.BlockSpec((None, rows, block), lambda j, m: (m, 0, which * steps + j)),
            pl.BlockSpec((rows, block), lambda j, m: (0, j)),
            pl.BlockSpec(memory_space=pl.ANY),
        ],
        out_specs=pl.BlockSpec((None, edge.shape[0], block), lambda j, m: (m, 0, j)),
        out_shape=jax.ShapeDtypeStruct((count, edge.shape[0], half), BF16),
        compiler_params=params(),
        cost_estimate=cost(edge.shape[0] * memb.size, memb.size),
        name="weighted_edge_sums",
    )(edge, memb, grad, after)


def filter_x_kernel(block, count, field_ref, *refs):
    weights, (spread_ref, block_ref), (out_ref, token_ref) = refs[:count], refs[count : count + 2], refs[-2:]
    field = field_ref[...]
    if weights:
        field = field * jnp.concatenate([ref[...] for ref in weights], axis=1)
    edges = dot(field, spread_ref[...]).astype(BF16)
    for start in range(0, field.shape[1], block):
        part = slice(start, start + block)
        both = jnp.concatenate([field[:, part], edges], axis=1)
        out_ref[:, part] = dot(both, block_ref[:, part]).astype(BF16)
    token_ref[...] = jnp.zeros_like(token_ref)


def filter_x(members, field, weights, spread_x, block_x, after):
    count, rows, columns = field.shape
    height = pick_block(rows, 384, 256, 128)
    block = block_x.shape[0] - LANES
    whole = lambda i, m: (0, 0)
    return pl.pallas_call(
        functools.partial(filter_x_kernel, block, len(weights)),
        grid=(rows // height, len(members)),
        in_specs=[
            pl.BlockSpec((None, height, columns), lambda i, m: (members[0] + m, i, 0)),
            *[pl.BlockSpec((height, columns // 2), lambda i, m: (i, 0)) for _ in weights],
            pl.BlockSpec(spread_x.shape, whole),
            pl.BlockSpec(block_x.shape, whole),
            *[pl.BlockSpec(memory_space=pl.ANY) for _ in after],
        ],
        out_specs=[
            pl.BlockSpec((None, height, columns), lambda i, m: (m, i, 0)),
            pl.BlockSpec((1, 2), whole),
        ],
        out_shape=[
            jax.ShapeDtypeStruct((len(members), rows, columns), BF16),
            jax.ShapeDtypeStruct((1, 2), F32),
        ],
        compiler_params=params(),
        cost_estimate=cost(
            2 * len(members) * rows * columns * (block + 2 * LANES), 2 * len(members) * rows * columns
        ),
        name="filter_x",
    )(field, *weights, spread_x, block_x, *after)


def halo_along_x(at, halo, sums, block_ref, block):
    part = halo[:, pl.ds(pl.multiple_of(at * block, block), block)]
    return dot(jnp.concatenate([part, sums], axis=1), block_ref[...]).astype(BF16)


def increment_kernel(
    block, first_ref, mix_ref, mix_halo_ref, memb_ref, halo_ref, spread_ref, block_ref, *refs
):
    count = memb_ref.shape[0]
    fields, out_ref, sums_ref = refs[:count], refs[-2], refs[-1]
    step = pl.program_id(0)

    @pl.when(step == 0)
    def _():
        for m in range(count):
            sums_ref[m] = dot(halo_ref[m], spread_ref[...]).astype(BF16)

    total = None
    for m in range(count):
        halo = halo_along_x(first_ref[0] + step, halo_ref.at[m], sums_ref[m], block_ref, block)
        shaped = dot(mix_ref[...], fields[m][...]) + dot(mix_halo_ref[...], halo)
        term = shaped * memb_ref[m].astype(F32)
        total = term if total is None else total + term
    out_ref[...] = total.astype(BF16)


def partial_increment(first, after, blocks, mix, mix_halo, fields, memb, halo, spread_x, block_x):
    count, rows, columns = memb.shape
    block = block_x.shape[0] - LANES
    pick = lambda j, first: (0, 0, first[0] + j)
    whole2 = lambda j, first: (0, 0)
    return pl.pallas_call(
        functools.partial(increment_kernel, block),
        grid_spec=pltpu.PrefetchScalarGridSpec(
            num_scalar_prefetch=1,
            grid=(blocks,),
            in_specs=[
                pl.BlockSpec(mix.shape, whole2),
                pl.BlockSpec(mix_halo.shape, whole2),
                pl.BlockSpec((count, rows, block), pick),
                pl.BlockSpec(halo.shape, lambda j, first: (0, 0, 0)),
                pl.BlockSpec(spread_x.shape, whole2),
                pl.BlockSpec((block_x.shape[0], block), lambda j, first: (0, first[0] + j)),
                *[pl.BlockSpec((None, rows, block), pick) for _ in fields],
                pl.BlockSpec(memory_space=pl.ANY),
            ],
            out_specs=pl.BlockSpec((rows, block), lambda j, first: (0, j)),
            scratch_shapes=[pltpu.VMEM((count, halo.shape[1], LANES), BF16)],
        ),
        out_shape=jax.ShapeDtypeStruct((rows, blocks * block), BF16),
        compiler_params=params(),
        cost_estimate=cost(
            2 * count * rows * (rows + halo.shape[1]) * blocks * block,
            2 * count * rows * blocks * block + rows * rows,
        ),
        name="partial_increment",
    )(first[None], mix, mix_halo, memb, halo, spread_x, block_x, *fields, after)


def join_kernel(own_ref, other_ref, after_ref, out_ref):
    out_ref[...] = (own_ref[...].astype(F32) + other_ref[...].astype(F32)).astype(BF16)


def join(own, other, after):
    rows, columns = own.shape
    height = pick_block(rows, 384, 256, 128)
    block = pl.BlockSpec((height, columns), lambda i: (i, 0))
    return pl.pallas_call(
        join_kernel,
        grid=(rows // height,),
        in_specs=[block, block, pl.BlockSpec(memory_space=pl.ANY)],
        out_specs=block,
        out_shape=jax.ShapeDtypeStruct(own.shape, BF16),
        compiler_params=params(),
        cost_estimate=cost(own.size, 3 * own.size),
        name="join",
    )(own, other, after)


def zero_kernel(*refs):
    refs[-1][...] = jnp.zeros_like(refs[-1])


def zero_after(*after):
    return pl.pallas_call(
        zero_kernel,
        in_specs=[pl.BlockSpec(memory_space=pl.ANY)] * len(after),
        out_shape=jax.ShapeDtypeStruct((1, 2), F32),
        name="zero_after",
    )(*after)


def hold_kernel(*refs):
    del refs


def hold(array, *after):
    return pl.pallas_call(
        hold_kernel,
        in_specs=[pl.BlockSpec(memory_space=pl.ANY)] * (1 + len(after)),
        out_specs=pl.BlockSpec(memory_space=pl.ANY),
        out_shape=jax.ShapeDtypeStruct(array.shape, array.dtype),
        input_output_aliases={0: 0},
        name="hold",
    )(array, *after)


def adjoint_inside_kernel(mix_ref, memb_ref, grad_ref, after_ref, out_ref):
    out_ref[...] = dot(mix_ref[...], memb_ref[...] * grad_ref[...]).astype(BF16)


def adjoint_inside(which, mix, memb, grad, after):
    count, rows, columns = memb.shape
    half = columns // 2
    block = pick_block(half, 768, 256, 128)
    steps = half // block
    return pl.pallas_call(
        adjoint_inside_kernel,
        grid=(steps, count),
        in_specs=[
            pl.BlockSpec(mix.shape, lambda j, m: (0, 0)),
            pl.BlockSpec((None, rows, block), lambda j, m: (m, 0, which * steps + j)),
            pl.BlockSpec((rows, block), lambda j, m: (0, j)),
            pl.BlockSpec(memory_space=pl.ANY),
        ],
        out_specs=pl.BlockSpec((None, rows, block), lambda j, m: (m, 0, j)),
        out_shape=jax.ShapeDtypeStruct((count, rows, half), BF16),
        compiler_params=params(),
        cost_estimate=cost(rows * memb.size, memb.size + rows * rows),
        name="adjoint_inside",
    )(mix, memb, grad, after)


def adjoint_kernel(
    block, left_ref, right_ref, mix_halo_ref, halo_ref, spread_ref, block_ref, out_ref
):
    inside = jnp.concatenate([left_ref[...], right_ref[...]], axis=1)
    field = (dot(mix_halo_ref[...], halo_ref[...]) + inside.astype(F32)).astype(BF16)
    edges = dot(field, spread_ref[...]).astype(BF16)
    for start in range(0, field.shape[1], block):
        part = slice(start, start + block)
        both = jnp.concatenate([field[:, part], edges], axis=1)
        out_ref[:, part] = dot(both, block_ref[:, part]).astype(BF16)


def adjoint_outside(left, right, mix_halo, halo, spread_x, block_x):
    count, rows, half = left.shape
    height = pick_block(rows, 384, 256, 128)
    block = block_x.shape[0] - LANES
    pick = lambda m, i: (m, i, 0)
    whole = lambda m, i: (0, 0)
    return pl.pallas_call(
        functools.partial(adjoint_kernel, block),
        grid=(count, rows // height),
        in_specs=[
            pl.BlockSpec((None, height, half), pick),
            pl.BlockSpec((None, height, half), pick),
            pl.BlockSpec((height, mix_halo.shape[1]), lambda m, i: (i, 0)),
            pl.BlockSpec((None,) + halo.shape[1:], lambda m, i: (m, 0, 0)),
            pl.BlockSpec(spread_x.shape, whole),
            pl.BlockSpec(block_x.shape, whole),
        ],
        out_specs=pl.BlockSpec((None, height, 2 * half), pick),
        out_shape=jax.ShapeDtypeStruct((count, rows, 2 * half), BF16),
        compiler_params=params(),
        cost_estimate=cost(4 * left.size * (block + 2 * LANES), 4 * left.size),
        name="adjoint_outside",
    )(left, right, mix_halo, halo, spread_x, block_x)


def hop_factors(tile, tiles, rows, step_y):
    hops = np.array([1 << k for k in range(tiles.bit_length() - 1)], np.int32)
    pair = tile - lax.rem(tile, 2)
    group = tile - lax.rem(jnp.broadcast_to(tile, hops.shape), hops)
    upper = lax.rem(lax.div(group, hops), np.int32(2)) == 1
    first = jnp.where(upper, group - hops, group)
    middle = first + hops
    base = jnp.where(hops == 1, tile, pair)
    after = jnp.where(hops == 1, tile + 1, pair + 2)
    frm = [middle * rows - 1, first * rows, middle * rows - 1, after * rows]
    to = [(middle + hops) * rows - 1, middle * rows, base * rows - 1, middle * rows]
    frm = jnp.concatenate(frm + [jnp.stack([pair * rows - 1, (tile + 1) * rows])])
    to = jnp.concatenate(to + [jnp.stack([tile * rows - 1, (pair + 2) * rows])])
    index = jnp.arange(step_y.shape[0], dtype=jnp.int32)[None]
    between = jnp.logical_and(index > frm[:, None], index <= to[:, None])
    factor = jnp.exp(-jnp.sum(jnp.where(between, step_y[None], 0.0), axis=1))
    end, start, below, above = [factor[k * len(hops) : (k + 1) * len(hops)] for k in range(4)]
    upper = upper.astype(F32)
    lower = 1.0 - upper
    ways = [
        upper + lower * end, upper * start + lower,
        upper * end + lower, upper + lower * start,
        upper * below, lower * above,
    ]
    return jnp.stack(ways, axis=1).reshape(len(hops), 3, 2), factor[4 * len(hops) :]


def outside(sums, tile, tiles, levels, factors, meanwhile):
    count, _, columns = sums.shape
    sums = sums.reshape(count, 2, levels, columns)
    part = count // 2
    odd = lax.rem(tile, 2)
    factor, way = factors

    def pair(x, hop):
        return lax.ppermute(x, "tile", [(s, s ^ hop) for s in range(tiles)])

    def by_way(pair_of):
        return pair_of.reshape(1, 2, 1, 1)

    other = pair(sums, 1)
    mine = lax.dynamic_slice_in_dim(sums, odd * part, part, 0).astype(F32)
    theirs = lax.dynamic_slice_in_dim(other, odd * part, part, 0).astype(F32)
    group = (by_way(factor[0, 0]) * mine + by_way(factor[0, 1]) * theirs).astype(BF16)
    token = meanwhile(0, other)
    far = jnp.zeros(group.shape, F32)
    hop, at = 2, 1
    while hop < tiles:
        enter = factor[at, 2]
        if 2 * hop < tiles:
            theirs = pair(group, hop)
            came = theirs
            keep = factor[at, 0]
            if token is not None:
                keep = keep + token[0]
            group = by_way(keep) * group.astype(F32) + by_way(factor[at, 1]) * theirs.astype(F32)
            group = group.astype(BF16)
        else:
            upper = lax.rem(lax.div(tile, hop), 2) == 1
            theirs = pair(jnp.where(upper, group[:, 1], group[:, 0]), hop)
            came = theirs[:, None]
            if token is not None:
                enter = enter + token[0]
        far += by_way(enter) * came.astype(F32)
        token = meanwhile(at, theirs)
        hop *= 2
        at += 1
    far = far.astype(BF16)
    there = pair(far, 1)
    far = jnp.where(
        odd == 0,
        jnp.concatenate([far, there], axis=0),
        jnp.concatenate([there, far], axis=0),
    )
    halo = far.astype(F32) * by_way(way) + other.astype(F32) * by_way(factor[0, 2])
    return halo.astype(BF16).reshape(count, 2 * levels, columns), theirs


def body(tiles, control, members, gradient, step_x, step_y, step_z):
    count, levels, rows, columns = control.shape
    flat = (count, levels * rows, columns)
    tile = lax.axis_index("tile")
    side = lax.axis_index("mem")
    half = columns // 2
    block = pick_block(half, 256, 128)
    owned = gradient.shape[0]
    def in_order(own, other, axis):
        return jnp.where(
            side == 0,
            jnp.concatenate([own, other], axis=axis),
            jnp.concatenate([other, own], axis=axis),
        )

    def to_rows(part):
        part = part.reshape(owned, tiles, rows, -1).swapaxes(0, 1).reshape(levels, rows, -1)
        return lax.all_to_all(part, "tile", 0, 0, tiled=True).reshape(levels * rows, -1)

    def to_levels(part):
        part = lax.all_to_all(part.reshape(levels, rows, -1), "tile", 0, 0, tiled=True)
        part = part.reshape(tiles, owned, rows, -1).swapaxes(0, 1)
        return part.reshape(owned, tiles * rows, -1)

    left = to_rows(gradient[:, :, :half])

    factors = hop_factors(tile, tiles, rows, step_y)
    field = control.reshape(flat)
    memb = members.reshape(flat)
    edge, control_sums = edge_sums(tile, step_y, levels, field)
    along, mixes, factors_x = [], [], []

    def prepare(k, came):
        if k == 0:
            factors_x.extend(prepare_x(step_x, block, came))
        if k < count:
            result, token = filter_x([k], field, (), *factors_x, (came,))
            along.append(result)
            return token
        if k == count:
            *result, token = prepare_y(tile, step_y, step_z, levels, levels * rows, came)
            mixes.extend(result)
            return token
        return None

    halo, last = outside(control_sums, tile, tiles, levels, factors, prepare)
    for k in range(len(along) + len(mixes) // 2, count + 1):
        prepare(k, last)
    mix, mix_halo = mixes
    spread_x, block_x = factors_x

    right = to_rows(hold(gradient[:, :, half:], last, mix))

    blocks = half // block
    sizes = CHUNKS if sum(CHUNKS) == blocks else [blocks]
    starts = [sum(sizes[:k]) for k in range(len(sizes))]
    share = functools.partial(
        partial_increment,
        mix=mix, mix_halo=mix_halo, fields=along, memb=memb, halo=halo, spread_x=spread_x,
        block_x=block_x,
    )
    sent, now = [], halo
    for at, size in zip(starts, sizes):
        now = share((1 - side) * blocks + at, now, blocks=size)
        sent.append(now)
    others = [lax.ppermute(x, "mem", SWAP) for x in sent]
    now = left_sums = weighted_edge_sums(0, edge, memb, left, now)
    mine, rest = [], []
    for k, (at, size) in enumerate(zip(starts, sizes)):
        now = own = share(side * blocks + at, now, blocks=size)
        if k == 0:
            now = right_sums = weighted_edge_sums(1, edge, memb, right, now)
        if k == len(sizes) - 1:
            now = left_inside = adjoint_inside(0, mix, memb, left, now)
        now = join(own, others[k], now)
        mine.append(to_levels(now))
        rest.append(lax.ppermute(mine[-1], "mem", SWAP))
    increment = in_order(jnp.concatenate(mine, axis=2), jnp.concatenate(rest, axis=2), 2)

    right_inside = adjoint_inside(1, mix, memb, right, now)
    hops = tiles.bit_length() - 1

    def wait(k, came):
        return zero_after(came, mine[0], right_inside) if k == hops - 3 else None

    weighted_sums = jnp.concatenate([left_sums, right_sums], axis=2)
    weighted_halo, _ = outside(weighted_sums, tile, tiles, levels, factors, wait)
    control_grad = adjoint_outside(
        left_inside, right_inside, mix_halo, weighted_halo, spread_x, block_x
    )
    return increment, control_grad.reshape(control.shape)


def solution(mesh):
    placed = (
        P("mem", None, "tile", None),
        P("mem", None, "tile", None),
        P("tile", None, None),
        P(),
        P(),
        P(),
    )
    return jax.shard_map(
        functools.partial(body, mesh.shape["tile"]),
        mesh=mesh,
        in_specs=placed,
        out_specs=(P("tile", None, None), P("mem", None, "tile", None)),
        check_vma=False,
    )
```
